128 devices in a mesh: tm: 16 (over y, z_lo, core), height: 8 (over z_hi, x).
Axes of the slice: x: 4, y: 4, z: 4 (z_hi: 2, z_lo: 2; z = z_hi * 2 + z_lo), core: 2. Of those that a mesh axis runs over, the one named last changes fastest.
Arguments:
- hidden: bfloat16 [32, 40, 80, 5120], P('tm', None, 'height'), may hold values from -256 to 256
- modulation: float32 [2, 4, 5120], replicated, may hold values from -3 to 3
- clip_lengths: int32 [4], replicated, may hold values from 1 to 10, 32 in all
- head_weight: bfloat16 [5120, 64], replicated, may hold values from -0.078125 to 0.078125
- head_bias: float32 [64], replicated, may hold values from -3 to 3
- conv_in_weight: bfloat16 [3, 3, 3, 16, 384], replicated, may hold values from -0.3125 to 0.3125
- conv_in_bias: float32 [384], replicated, may hold values from -3 to 3
- conv_out_weight: bfloat16 [3, 3, 3, 384, 384], replicated, may hold values from -0.0625 to 0.0625
- conv_out_bias: float32 [384], replicated, may hold values from -3 to 3
Outputs:
- decoded: bfloat16 [32, 80, 160, 384], P('tm', 'height')
The draws below stay inside these ranges and needn't reach their ends.
Inputs may be any that keep to these rules, and one draw needn't show every extreme that they name: `clip_lengths`: clip lengths in frames; they sum to 32 and the longest is exactly 10.
All inputs are finite; a program needn't handle non-finite values.
Results may differ from the reference program's by a relative error of at most 0.0057.
Values may be sent and summed in bfloat16 or wider, within the bound.
A program may use at most 192 MiB of HBM per device.

```python
import math
import jax
import jax.numpy as jnp
import numpy as np
from jax import lax

D = 5120
ZCH = 16
CH = 384
F_DEV = 2
CLIPS = 4
FRAMES = 32
TROWS = 40
TCOLS = 80
LONGEST = 10


def draw_hidden(key, part):
    key = jax.random.fold_in(key, 11)
    key_values, key_rows, key_cols, key_offset = jax.random.split(key, 4)
    shape = (FRAMES, TROWS, TCOLS, D)
    base = jax.random.truncated_normal(key_values, -4.0, 4.0, shape, jnp.float32)
    row_scale = jnp.exp(jax.random.uniform(key_rows, (FRAMES, TROWS, TCOLS, 1), jnp.float32, 0.0, math.log(10.0)))
    col_scale = jnp.exp(jax.random.uniform(key_cols, (D,), jnp.float32, math.log(0.3), math.log(3.0)))
    offset = 0.5 * jax.random.truncated_normal(jax.random.fold_in(key_offset, 5), -3.0, 3.0, (FRAMES, TROWS, TCOLS, 1), jnp.float32)
    return ((base * col_scale + offset) * row_scale).astype(jnp.bfloat16)


def length_profile(amount, total, reach, slope):
    portions = [(1 << 20) // math.isqrt(grade ** slope) + 1 for grade in range(2, amount + 1)]
    rest, holding = total - reach - (amount - 1), [1] * (amount - 1)
    while rest > 0:
        free = [i for i in range(amount - 1) if holding[i] < reach]
        mass, remaining = sum([portions[i] for i in free]), rest
        for i in free:
            more = min(reach - holding[i], max(1, remaining * portions[i] // mass), rest)
            holding[i] = holding[i] + more
            rest = rest - more
    return np.array([reach] + holding)


def ragged(stream_key, amount, total, bound, slope):
    if amount == 2:
        one = jax.random.randint(stream_key, (), max(1, total - bound), min(bound, total - 1) + 1)
        return jnp.stack([one, total - one])
    sizes = jnp.asarray(length_profile(amount, total, bound, slope), jnp.int32)
    pairs = (amount - 1) // 2
    donor, receiver = sizes[1:1 + 2 * pairs:2], sizes[2:2 + 2 * pairs:2]
    slack = jnp.minimum(donor - 1, bound - receiver)
    shifted = jax.random.randint(jax.random.fold_in(stream_key, 1), (pairs,), 0, 1 << 20) % (slack + 1)
    sizes = sizes.at[1:1 + 2 * pairs:2].set(donor - shifted).at[2:2 + 2 * pairs:2].set(receiver + shifted)
    return sizes[jax.random.permutation(jax.random.fold_in(stream_key, 2), amount)]


def scatter_about(own_key, shape, scale, reach, kind=jnp.bfloat16):
    drawn = jax.random.normal(own_key, shape, jnp.float32) * scale
    return jnp.minimum(jnp.maximum(drawn, -reach), reach).astype(kind)


def setup_inputs(seed: int = 0) -> dict:
    key_of = jax.random.split(jax.random.key(seed), 10)
    return {
        "hidden": draw_hidden(jax.random.fold_in(key_of[9], 71), 0),
        "modulation": scatter_about(key_of[1], (2, CLIPS, D), 0.5, 3.0, jnp.float32),
        "clip_lengths": ragged(key_of[2], CLIPS, FRAMES, LONGEST, 2).astype(jnp.int32),
        "head_weight": scatter_about(key_of[3], (D, 4 * ZCH), D ** -0.5, 0.078125),
        "head_bias": scatter_about(key_of[4], (4 * ZCH,), 0.5, 3.0, jnp.float32),
        "conv_in_weight": scatter_about(key_of[5], (3, 3, 3, ZCH, CH), (27 * ZCH) ** -0.5, 0.3125),
        "conv_in_bias": scatter_about(key_of[6], (CH,), 0.5, 3.0, jnp.float32),
        "conv_out_weight": scatter_about(key_of[7], (3, 3, 3, CH, CH), (27 * CH) ** -0.5, 0.0625),
        "conv_out_bias": scatter_about(key_of[8], (CH,), 0.5, 3.0, jnp.float32),
    }


def clip_tables(clip_lengths, frame_ids):
    clip_ends = jnp.cumsum(clip_lengths).astype(jnp.int32)
    clip_starts = (clip_ends - clip_lengths).astype(jnp.int32)
    in_clip = (frame_ids[:, None] >= clip_starts[None, :]) & (frame_ids[:, None] < clip_ends[None, :])
    clip_first = lax.optimization_barrier(jnp.sum(jnp.where(in_clip, clip_starts[None, :], 0), axis=1)).astype(jnp.int32)
    return (in_clip, clip_first)

def frame_keep(frame_ids, clip_first):
    tap_offsets = jnp.arange(3, dtype=jnp.int32)
    return (frame_ids[None, :] - 2 + tap_offsets[:, None] >= clip_first[None, :]).astype(jnp.bfloat16)

def modulate_rows(in_clip, modulation):
    picked = in_clip.astype(jnp.float32)
    return lax.optimization_barrier(jnp.sum(picked[None, :, :, None] * modulation[:, None, :, :], axis=2))

def final_head(tokens, shift_rows, scale_rows, head_weight, head_bias):
    values = tokens.astype(jnp.float32)
    mean_value = lax.optimization_barrier(jnp.mean(values, axis=-1, keepdims=True))
    centred = values - mean_value
    variance = lax.optimization_barrier(jnp.mean(centred * centred, axis=-1, keepdims=True))
    normed = centred * lax.rsqrt(variance + 1e-06) * (1.0 + scale_rows[:, None, None, :]) + shift_rows[:, None, None, :]
    normed = normed.astype(jnp.bfloat16)
    lead_shape = normed.shape[:-1]
    projected = jnp.dot(normed.reshape(-1, normed.shape[-1]), head_weight, preferred_element_type=jnp.float32) + head_bias
    return projected.astype(jnp.bfloat16).reshape(lead_shape + (head_weight.shape[1],))

def unpatchify(latent_tokens):
    frame_count, row_count, col_count, width = latent_tokens.shape
    channels = width // 4
    shaped = latent_tokens.reshape(frame_count, row_count, col_count, 2, 2, channels)
    return shaped.transpose(0, 1, 3, 2, 4, 5).reshape(frame_count, 2 * row_count, 2 * col_count, channels)

def causal_conv(extended, weight, keep_mask):
    frame_count = extended.shape[0] - 2
    row_count = extended.shape[1] - 2
    col_count = extended.shape[2]
    channels = extended.shape[3]
    if 27 * channels <= 512:
        col_padded = jnp.pad(extended, ((0, 0), (0, 0), (1, 1), (0, 0)))
        pieces = []
        for time_tap in range(3):
            masked_slab = col_padded[time_tap:time_tap + frame_count] * keep_mask[time_tap][:, None, None, None]
            for row_tap in range(3):
                for col_tap in range(3):
                    pieces.append(masked_slab[:, row_tap:row_tap + row_count, col_tap:col_tap + col_count])
        tap_block = jnp.concatenate(pieces, axis=-1).reshape(-1, 27 * channels)
        total = jnp.dot(tap_block, weight.reshape(27 * channels, -1), preferred_element_type=jnp.float32)
        return total.reshape(frame_count, row_count, col_count, -1)
    total = jnp.zeros((frame_count, row_count, col_count, weight.shape[-1]), jnp.float32)
    for time_tap in range(3):
        masked_slab = extended[time_tap:time_tap + frame_count] * keep_mask[time_tap][:, None, None, None]
        total = total + lax.conv_general_dilated(masked_slab, weight[time_tap], (1, 1), ((0, 0), (1, 1)), dimension_numbers=('NHWC', 'HWIO', 'NHWC'), preferred_element_type=jnp.float32)
    return total

def whole_conv(grid, weight, keep_mask):
    padded = jnp.pad(grid, ((2, 0), (1, 1), (0, 0), (0, 0)))

    def one_block(block_index):
        start = block_index * F_DEV
        frame_block = lax.dynamic_slice_in_dim(padded, start, F_DEV + 2, 0)
        block_keep = lax.dynamic_slice_in_dim(keep_mask, start, F_DEV, 1)
        return causal_conv(frame_block, weight, block_keep)
    blocks = lax.map(one_block, jnp.arange(FRAMES // F_DEV, dtype=jnp.int32))
    return blocks.reshape((FRAMES,) + blocks.shape[2:])

def reference(hidden, modulation, clip_lengths, head_weight, head_bias, conv_in_weight, conv_in_bias, conv_out_weight, conv_out_bias):
    frame_ids = jnp.arange(FRAMES, dtype=jnp.int32)
    in_clip, clip_first = clip_tables(clip_lengths, frame_ids)
    modulated = modulate_rows(in_clip, modulation)

    def head_frame(items):
        frame_tokens, shift_row, scale_row = items
        return final_head(frame_tokens[None], shift_row[None], scale_row[None], head_weight, head_bias)[0]
    latent_tokens = lax.map(head_frame, (hidden, modulated[0], modulated[1]))
    latent_grid = unpatchify(latent_tokens)
    keep_mask = frame_keep(frame_ids, clip_first)
    inner_act = jax.nn.silu(whole_conv(latent_grid, conv_in_weight, keep_mask) + conv_in_bias).astype(jnp.bfloat16)
    decoded = whole_conv(inner_act, conv_out_weight, keep_mask) + conv_out_bias
    return decoded.astype(jnp.bfloat16)
```

```python
import functools

import jax
import jax.numpy as jnp
from jax import lax
from jax.experimental import pallas as pl
from jax.experimental.pallas import tpu as pltpu
from jax.sharding import PartitionSpec as P

F32 = jnp.float32
BF16 = jnp.bfloat16
MESH = pl.DeviceIdType.MESH


def clip_start(clip_ref, frame):
    first = jnp.int32(0)
    end = jnp.int32(0)
    for clip in range(clip_ref.shape[0] - 1):
        end = end + clip_ref[clip]
        first = jnp.where(frame >= end, end, first)
    return first


def conv_kernel(
    clip_ref, recv_ref, win_ref, bin_ref, wout_ref, bout_ref, out_ref,
    spread, tokens, dense_in, inner, raw, mixed, total, stage, packed, load_sem, store_sem,
    *, rows_per_step,
):
    slab = lax.axis_index("tm")
    band = lax.axis_index("height")
    frame0 = 2 * slab

    loads = []
    for part in range(9):
        cp = pltpu.make_async_copy(
            wout_ref.at[pl.ds(3 * part, 3)], raw.at[pl.ds(3 * part, 3)], load_sem.at[part]
        )
        cp.start()
        loads.append(cp)

    blank = jnp.zeros((16, 384), BF16)
    for a in range(3):
        for rr in range(4):
            for slot in range(4):
                for p in range(2):
                    for s in range(2):
                        b, e = rr - p, slot - s
                        ok = 0 <= b < 3 and 0 <= e < 3
                        row = a * 256 + rr * 64 + slot * 16
                        col = (2 * p + s) * 384
                        dense_in[row : row + 16, col : col + 384] = (
                            win_ref[9 * a + 3 * b + e] if ok else blank
                        )

    lane_in = lax.broadcasted_iota(jnp.int32, (128, 256), 0)
    lane_out = lax.broadcasted_iota(jnp.int32, (128, 256), 1)
    wanted = (
        (lane_out // 128) * 64
        + ((lane_out // 64) % 2) * 32
        + ((lane_out // 16 + 1) % 2) * 16
        + lane_out % 16
    )
    spreader = jnp.where(lane_in == wanted, 1.0, 0.0).astype(BF16)
    slot_id = (lax.broadcasted_iota(jnp.int32, (7, 10, 8, 128), 3) // 16) % 4
    group_id = lax.broadcasted_iota(jnp.int32, (7, 1, 8, 128), 2)
    for back in range(3):
        for src in range(8):
            block = recv_ref[back, src].astype(F32)
            for col in range(10):
                spread[back, pl.ds(8 * col + src, 8, stride=80), :] = block[8 * col : 8 * col + 8]
    for back in range(3):
        both = jnp.dot(spread[back, 0:560, :].astype(BF16), spreader, preferred_element_type=F32)
        for f in range(2):
            here = both[:, 128 * f : 128 * f + 128].reshape(7, 10, 8, 128)
            last = pltpu.roll(here[:, 9:10].reshape(56, 128), 1, 0).reshape(7, 1, 8, 128)
            last = jnp.where(group_id == 0, 0.0, last)
            head = pltpu.roll(here[:, 0:1].reshape(56, 128), 55, 0).reshape(7, 1, 8, 128)
            head = jnp.where(group_id == 7, 0.0, head)
            before = jnp.concatenate([last, here[:, 0:9]], axis=1)
            after = jnp.concatenate([here[:, 1:10], head], axis=1)
            mixed_slots = jnp.where(slot_id == 0, before, jnp.where(slot_id == 3, after, here))
            tokens[2 * back + f] = mixed_slots.reshape(560, 128).astype(BF16)

    keep = []
    for g in range(4):
        first = clip_start(clip_ref, frame0 - 2 + g)
        keep.append([frame0 - 4 + g + a >= first for a in range(3)])
    first0 = clip_start(clip_ref, frame0)
    use0 = frame0 - 2 >= first0
    use1 = frame0 - 1 >= first0
    joined = frame0 >= clip_start(clip_ref, frame0 + 1)
    c = jnp.where(joined, 1.0, 0.0).astype(F32)
    bias_in = bin_ref[...].reshape(1, 384)
    bias_in = jnp.concatenate([bias_in, bias_in], axis=1)

    def in_step(step, carry):
        i0 = 2 * step
        for p in range(2):
            x = []
            for g in range(4):
                parts = []
                for a in range(3):
                    lo = tokens[g + a, pl.ds(pl.multiple_of(i0 * 80, 16), 160), :]
                    hi = tokens[g + a, pl.ds(pl.multiple_of(i0 * 80 + 80, 16), 160), :]
                    both = jnp.concatenate([lo, hi], axis=1)
                    if a < 2:
                        both = jnp.where(keep[g][a], both, jnp.zeros_like(both))
                    parts.append(both)
                v = jnp.dot(
                    jnp.concatenate(parts, axis=1),
                    dense_in[:, 768 * p : 768 * p + 768],
                    preferred_element_type=F32,
                )
                v = 0.5 * (v + bias_in)
                v = v + v * jnp.tanh(v)
                x.append(v.astype(BF16).astype(F32))
            x0 = jnp.where(use0, x[0], 0.0)
            x1 = jnp.where(use1, x[1], 0.0)
            x2, x3 = x[2], x[3]
            sums = (x0 - c * x2, x1 + c * x2, x2 - c * x1, x3 - c * x1)
            for r in range(2):
                local = 4 * step + 2 * r + p
                h = 10 * band - 1 + local
                inside = jnp.logical_and(h >= 0, h < 80)
                for i in range(4):
                    part = sums[i][80 * r : 80 * r + 80]
                    inner[i, local] = jnp.where(inside, part, 0.0).astype(BF16)
        return carry

    lax.fori_loop(0, 3, in_step, 0)

    for cp in loads:
        cp.wait()

    def mix(k, carry):
        w0 = raw[k].astype(F32)
        w1 = raw[9 + k].astype(F32)
        w2 = raw[18 + k].astype(F32)
        outer = 0.5 * (w0 + w2)
        mid = 0.5 * w1
        mixed[0, k] = jnp.where(joined, outer + mid, w1).astype(BF16)
        mixed[1, k] = jnp.where(joined, outer - mid, w2).astype(BF16)
        return carry

    lax.fori_loop(0, 9, mix, 0)

    R = rows_per_step
    rows = 80 * R
    bias_out = bout_ref[...].reshape(1, 384)
    group_out = lax.broadcasted_iota(jnp.int32, (R, 1, 8, 384), 2)

    def weight(i, b, e):
        k = 3 * b + e
        if i == 0:
            return raw[k]
        if i == 3:
            return raw[18 + k]
        return mixed[i - 1, k]

    def product(i, h0):
        taps = [inner[i, pl.ds(h0 + b, R)].reshape(rows, 768) for b in range(3)]
        main_w = jnp.concatenate(
            [
                jnp.concatenate(
                    [
                        jnp.concatenate([weight(i, b, 1), weight(i, b, 0)], axis=1),
                        jnp.concatenate([weight(i, b, 2), weight(i, b, 1)], axis=1),
                    ],
                    axis=0,
                )
                for b in range(3)
            ],
            axis=0,
        )
        main = jnp.dot(jnp.concatenate(taps, axis=1), main_w, preferred_element_type=F32)
        left = jnp.dot(
            jnp.concatenate([tap[:, 384:] for tap in taps], axis=1),
            jnp.concatenate([weight(i, b, 0) for b in range(3)], axis=0),
            preferred_element_type=F32,
        )
        right = jnp.dot(
            jnp.concatenate([tap[:, :384] for tap in taps], axis=1),
            jnp.concatenate([weight(i, b, 2) for b in range(3)], axis=0),
            preferred_element_type=F32,
        )
        return (main, left, right)

    def finish(f, h0, main, left, right):
        left = left.reshape(R, 10, 8, 384)
        last = pltpu.roll(left[:, 9:10].reshape(8 * R, 384), 1, 0).reshape(R, 1, 8, 384)
        last = jnp.where(group_out == 0, 0.0, last)
        left = jnp.concatenate([last, left[:, 0:9]], axis=1).reshape(rows, 384)
        right = right.reshape(R, 10, 8, 384)
        head = pltpu.roll(right[:, 0:1].reshape(8 * R, 384), 8 * R - 1, 0).reshape(R, 1, 8, 384)
        head = jnp.where(group_out == 7, 0.0, head)
        right = jnp.concatenate([right[:, 1:10], head], axis=1).reshape(rows, 384)
        halves = (main[:, :384] + left + bias_out, main[:, 384:] + right + bias_out)
        for r in range(R):
            for s in range(2):
                for col in range(10):
                    at = 80 * r + 8 * col
                    for lane in range(3):
                        stage[f, 3 * r + lane, pl.ds(2 * col + s, 8, stride=20), :] = halves[s][
                            at : at + 8, 128 * lane : 128 * lane + 128
                        ]
        for r in range(R):
            for lane in range(3):
                packed[f, h0 + r, :, 128 * lane : 128 * lane + 128] = stage[
                    f, 3 * r + lane
                ].astype(BF16)

    def store(f, h0):
        return pltpu.make_async_copy(
            packed.at[f, pl.ds(h0, R)], out_ref.at[f, pl.ds(h0, R)], store_sem.at[f]
        )

    def out_step(step, carry):
        h0 = step * R
        m1 = product(1, h0)
        m2 = product(2, h0)
        at = (0, 768, 1152, 1536)
        for n, (u, v) in enumerate(zip(m1, m2)):
            total[0, :, at[n] : at[n + 1]] = u + v
            total[1, :, at[n] : at[n + 1]] = c * (u - v)
        for f in range(2):
            m = product(3 * f, h0)
            m = [total[f, :, at[n] : at[n + 1]] + u for n, u in enumerate(m)]
            finish(f, h0, *m)
            store(f, h0).start()
        return carry

    lax.fori_loop(0, 10 // R, out_step, 0)
    for f in range(2):
        pltpu.make_async_copy(packed.at[f], out_ref.at[f], store_sem.at[f]).wait()


def convolve(clip_lengths, received, conv_in_weight, conv_in_bias, conv_out_weight, conv_out_bias,
             rows_per_step=2):
    R = rows_per_step
    return pl.pallas_call(
        functools.partial(conv_kernel, rows_per_step=R),
        out_shape=jax.ShapeDtypeStruct((2, 10, 160, 384), BF16),
        in_specs=[
            pl.BlockSpec(memory_space=pltpu.SMEM),
            pl.BlockSpec(memory_space=pltpu.VMEM),
            pl.BlockSpec(memory_space=pltpu.VMEM),
            pl.BlockSpec(memory_space=pltpu.VMEM),
            pl.BlockSpec(memory_space=pl.ANY),
            pl.BlockSpec(memory_space=pltpu.VMEM),
        ],
        out_specs=pl.BlockSpec(memory_space=pl.ANY),
        scratch_shapes=[
            pltpu.VMEM((3, 640, 128), F32),
            pltpu.VMEM((6, 560, 128), BF16),
            pltpu.VMEM((768, 1536), BF16),
            pltpu.VMEM((4, 12, 80, 768), BF16),
            pltpu.VMEM((27, 384, 384), BF16),
            pltpu.VMEM((2, 9, 384, 384), BF16),
            pltpu.VMEM((2, 80 * R, 1536), F32),
            pltpu.VMEM((2, 3 * R, 160, 128), F32),
            pltpu.VMEM((2, 10, 160, 384), BF16),
            pltpu.SemaphoreType.DMA((9,)),
            pltpu.SemaphoreType.DMA((2,)),
        ],
        compiler_params=pltpu.CompilerParams(vmem_limit_bytes=60 << 20),
    )(
        clip_lengths,
        received,
        conv_in_weight.reshape(27, 16, 384),
        conv_in_bias,
        conv_out_weight.reshape(27, 384, 384),
        conv_out_bias,
    )


def head_kernel(
    clip_ref, hidden_ref, mod_ref, weight_ref, bias_ref, recv_ref,
    tokens, rhs, aux, raw, grid, outgoing, load_sem, send_sem, recv_sem,
):
    slab = lax.axis_index("tm")
    band = lax.axis_index("height")
    slabs = lax.axis_size("tm")
    bands = lax.axis_size("height")

    barrier = pltpu.get_barrier_semaphore()
    for d in range(3):
        for o in range(bands):
            if d or o:
                source = (lax.rem(slab + slabs - d, slabs), lax.rem(band + bands - o, bands))
                pl.semaphore_signal(barrier, inc=1, device_id=source, device_id_type=MESH)

    def load(n):
        return pltpu.make_async_copy(
            hidden_ref.at[pl.ds(pl.multiple_of(160 * n, 16), 160)], tokens.at[n], load_sem.at[n]
        )

    for n in range(5):
        load(n).start()

    weight = weight_ref[...].astype(F32)
    row_id = lax.broadcasted_iota(jnp.int32, (16, 5120), 0)
    extra = jnp.where(row_id == 0, 1.0, 0.0)
    for f in range(2):
        frame = 2 * slab + f
        end = jnp.int32(0)
        shift, scale = mod_ref[0, 0:1, :], mod_ref[1, 0:1, :]
        for clip in range(1, clip_ref.shape[0]):
            end = end + clip_ref[clip - 1]
            later = frame >= end
            shift = jnp.where(later, mod_ref[0, clip : clip + 1, :], shift)
            scale = jnp.where(later, mod_ref[1, clip : clip + 1, :], scale)
        rhs[64 * f : 64 * f + 64, :] = (weight * (1.0 + scale)).astype(BF16)
        rhs[128 + 64 * f : 192 + 64 * f, :] = weight_ref[...]
        coarse = shift.astype(BF16).astype(F32)
        extra = jnp.where(row_id == 2 * f + 1, coarse, extra)
        extra = jnp.where(row_id == 2 * f + 2, shift - coarse, extra)
    aux[...] = extra.astype(BF16)
    contract = (((1,), (1,)), ((), ()))
    sums = lax.dot_general(aux[...], rhs[...], contract, preferred_element_type=F32)
    lane = lax.broadcasted_iota(jnp.int32, (1, 128), 1)
    head_bias = bias_ref[...].reshape(1, 64)
    col_sum = sums[0:1, 0:128]
    offset = (
        jnp.where(lane < 64, sums[1:2, 128:] + sums[2:3, 128:], sums[3:4, 128:] + sums[4:5, 128:])
        + jnp.concatenate([head_bias, head_bias], axis=1)
    )

    zeros = jnp.zeros((8, 128), F32)
    for q in range(20):
        grid[56 * q : 56 * q + 8, :] = zeros
        grid[56 * q + 48 : 56 * q + 56, :] = zeros

    def head_step(n, carry):
        load(n).wait()
        raw[...] = lax.dot_general(
            tokens[n], rhs[0:128, :], contract, preferred_element_type=F32
        )

        def strip_step(k, inner_carry):
            at = pl.ds(pl.multiple_of(16 * k, 16), 16)
            pivot = jnp.sum(tokens[n, at, 0:128].astype(F32), axis=1, keepdims=True) / 128.0
            first = jnp.zeros((16, 128), F32)
            second = jnp.zeros((16, 128), F32)
            for tile in range(40):
                v = tokens[n, at, 128 * tile : 128 * tile + 128].astype(F32) - pivot
                first = first + v
                second = second + v * v
            first = jnp.sum(first, axis=1, keepdims=True) / 5120.0
            second = jnp.sum(second, axis=1, keepdims=True) / 5120.0
            scale = lax.rsqrt(second - first * first + 1e-06)
            value = scale * (raw[at, :] - (pivot + first) * col_sum) + offset
            for half in range(2):
                m = 20 * n + 2 * k + half
                row = (m // 5) * 56 + 8 + (m % 5) * 8
                grid[pl.ds(pl.multiple_of(row, 8), 8), :] = value[8 * half : 8 * half + 8]
            return inner_carry

        return lax.fori_loop(0, 10, strip_step, carry)

    lax.fori_loop(0, 5, head_step, 0)

    lane8 = lax.broadcasted_iota(jnp.int32, (8, 128), 1)
    for j in range(8):
        for pair in range(5):
            pieces = []
            for q in (2 * pair, 2 * pair + 1):
                at = 56 * q + 7 + 5 * j
                pieces.append(
                    jnp.where(lane8 < 64, grid[at : at + 8, :], grid[560 + at : 568 + at, :])
                )
            outgoing[j, 16 * pair : 16 * pair + 16, :] = jnp.concatenate(pieces, axis=0).astype(
                BF16
            )

    pl.semaphore_wait(barrier, 3 * bands - 1)
    copies = []
    for o in range(bands):
        to = lax.rem(band + o, bands)
        for d in range(3):
            target = recv_ref.at[2 - d, band]
            if d or o:
                cp = pltpu.make_async_remote_copy(
                    src_ref=outgoing.at[to],
                    dst_ref=target,
                    send_sem=send_sem.at[d, o],
                    recv_sem=recv_sem.at[d, o],
                    device_id=(lax.rem(slab + d, slabs), to),
                    device_id_type=MESH,
                )
            else:
                cp = pltpu.make_async_copy(outgoing.at[to], target, send_sem.at[d, o])
            cp.start()
            copies.append(cp)
    for cp in copies:
        cp.wait()


def head(clip_lengths, hidden, modulation, head_weight, head_bias):
    return pl.pallas_call(
        head_kernel,
        out_shape=jax.ShapeDtypeStruct((3, 8, 80, 128), BF16),
        in_specs=[
            pl.BlockSpec(memory_space=pltpu.SMEM),
            pl.BlockSpec(memory_space=pl.ANY),
            pl.BlockSpec(memory_space=pltpu.VMEM),
            pl.BlockSpec(memory_space=pltpu.VMEM),
            pl.BlockSpec(memory_space=pltpu.VMEM),
        ],
        out_specs=pl.BlockSpec(memory_space=pl.ANY),
        scratch_shapes=[
            pltpu.VMEM((5, 160, 5120), BF16),
            pltpu.VMEM((256, 5120), BF16),
            pltpu.VMEM((16, 5120), BF16),
            pltpu.VMEM((160, 128), F32),
            pltpu.VMEM((1120, 128), F32),
            pltpu.VMEM((8, 80, 128), BF16),
            pltpu.SemaphoreType.DMA((5,)),
            pltpu.SemaphoreType.DMA((3, 8)),
            pltpu.SemaphoreType.DMA((3, 8)),
        ],
        compiler_params=pltpu.CompilerParams(
            collective_id=0, has_side_effects=True, vmem_limit_bytes=60 << 20
        ),
    )(
        clip_lengths,
        hidden.transpose(0, 2, 1, 3).reshape(800, 5120),
        modulation,
        head_weight.T,
        head_bias,
    )


def on_device(
    hidden, modulation, clip_lengths, head_weight, head_bias,
    conv_in_weight, conv_in_bias, conv_out_weight, conv_out_bias,
):
    received = head(clip_lengths, hidden, modulation, head_weight, head_bias)
    return convolve(
        clip_lengths, received, conv_in_weight, conv_in_bias, conv_out_weight, conv_out_bias
    )


def solution(mesh):
    return jax.shard_map(
        on_device,
        mesh=mesh,
        in_specs=(P("tm", None, "height", None), P(), P(), P(), P(), P(), P(), P(), P()),
        out_specs=P("tm", "height", None, None),
        check_vma=False,
    )
```

```python
import functools

import jax
import jax.numpy as jnp
from jax import lax
from jax.experimental import pallas as pl
from jax.experimental.pallas import tpu as pltpu
from jax.sharding import PartitionSpec as P

F32 = jnp.float32
BF16 = jnp.bfloat16
MESH = pl.DeviceIdType.MESH


def clip_start(clip_ref, frame):
    first = jnp.int32(0)
    end = jnp.int32(0)
    for clip in range(clip_ref.shape[0] - 1):
        end = end + clip_ref[clip]
        first = jnp.where(frame >= end, end, first)
    return first


def conv_kernel(
    clip_ref, recv_ref, dense_ref, bin_ref, wout_ref, mixed_ref, bout_ref, out_ref,
    received, spread, tokens, dense_in, inner, weights, total, stage, packed,
    recv_sem, load_sem, store_sem, *, rows_per_step,
):
    slab = lax.axis_index("tm")
    band = lax.axis_index("height")
    frame0 = 2 * slab

    recv_copy = pltpu.make_async_copy(recv_ref, received, recv_sem)
    recv_copy.start()
    dense_copy = pltpu.make_async_copy(dense_ref, dense_in, load_sem.at[4])
    dense_copy.start()
    sources = (
        wout_ref.at[pl.ds(0, 9)], mixed_ref.at[0], mixed_ref.at[1], wout_ref.at[pl.ds(18, 9)]
    )
    loads = [
        pltpu.make_async_copy(sources[i], weights.at[i], load_sem.at[i]) for i in range(4)
    ]

    lane_in = lax.broadcasted_iota(jnp.int32, (128, 256), 0)
    lane_out = lax.broadcasted_iota(jnp.int32, (128, 256), 1)
    wanted = (
        (lane_out // 128) * 64
        + ((lane_out // 64) % 2) * 32
        + ((lane_out // 16 + 1) % 2) * 16
        + lane_out % 16
    )
    spreader = jnp.where(lane_in == wanted, 1.0, 0.0).astype(BF16)
    slot_id = (lax.broadcasted_iota(jnp.int32, (7, 10, 8, 128), 3) // 16) % 4
    group_id = lax.broadcasted_iota(jnp.int32, (7, 1, 8, 128), 2)
    recv_copy.wait()
    for back in range(3):
        for src in range(8):
            block = received[back, src].astype(F32)
            for col in range(10):
                spread[back, pl.ds(8 * col + src, 8, stride=80), :] = block[8 * col : 8 * col + 8]
    for back in range(3):
        both = jnp.dot(spread[back, 0:560, :].astype(BF16), spreader, preferred_element_type=F32)
        for f in range(2):
            here = both[:, 128 * f : 128 * f + 128].reshape(7, 10, 8, 128)
            last = pltpu.roll(here[:, 9:10].reshape(56, 128), 1, 0).reshape(7, 1, 8, 128)
            last = jnp.where(group_id == 0, 0.0, last)
            head = pltpu.roll(here[:, 0:1].reshape(56, 128), 55, 0).reshape(7, 1, 8, 128)
            head = jnp.where(group_id == 7, 0.0, head)
            before = jnp.concatenate([last, here[:, 0:9]], axis=1)
            after = jnp.concatenate([here[:, 1:10], head], axis=1)
            mixed_slots = jnp.where(slot_id == 0, before, jnp.where(slot_id == 3, after, here))
            tokens[2 * back + f] = mixed_slots.reshape(560, 128).astype(BF16)

    keep = []
    for g in range(4):
        first = clip_start(clip_ref, frame0 - 2 + g)
        keep.append([frame0 - 4 + g + a >= first for a in range(3)])
    first0 = clip_start(clip_ref, frame0)
    use0 = frame0 - 2 >= first0
    use1 = frame0 - 1 >= first0
    joined = frame0 >= clip_start(clip_ref, frame0 + 1)
    c = jnp.where(joined, 1.0, 0.0).astype(F32)
    c16 = c.astype(BF16)
    bias_in = 0.5 * bin_ref[...].reshape(1, 384)
    bias_in = jnp.concatenate([bias_in, bias_in], axis=1)
    dense_copy.wait()
    for i in (1, 2, 0, 3):
        loads[i].start()

    def in_step(step, carry):
        i0 = 2 * step
        for p in range(2):
            x = []
            for g in range(4):
                parts = []
                for a in range(3):
                    lo = tokens[g + a, pl.ds(pl.multiple_of(i0 * 80, 16), 160), :]
                    hi = tokens[g + a, pl.ds(pl.multiple_of(i0 * 80 + 80, 16), 160), :]
                    both = jnp.concatenate([lo, hi], axis=1)
                    if a < 2:
                        both = jnp.where(keep[g][a], both, jnp.zeros_like(both))
                    parts.append(both)
                v = jnp.dot(
                    jnp.concatenate(parts, axis=1),
                    dense_in[:, 768 * p : 768 * p + 768],
                    preferred_element_type=F32,
                )
                v = v + bias_in
                x.append((v + v * jnp.tanh(v)).astype(BF16))
            zero = jnp.zeros_like(x[0])
            x0 = jnp.where(use0, x[0], zero)
            x1 = jnp.where(use1, x[1], zero)
            x2, x3 = x[2], x[3]
            x1c, x2c = c16 * x1, c16 * x2
            sums = (x0 - x2c, x1 + x2c, x2 - x1c, x3 - x1c)
            for r in range(2):
                for i in range(4):
                    inner[i, 4 * step + 2 * r + p] = sums[i][80 * r : 80 * r + 80]
        return carry

    lax.fori_loop(0, 3, in_step, 0)

    @pl.when(band == 0)
    def _():
        inner[:, 0] = jnp.zeros((4, 80, 768), BF16)

    @pl.when(band == 7)
    def _():
        inner[:, 11] = jnp.zeros((4, 80, 768), BF16)

    for cp in loads:
        cp.wait()

    R = rows_per_step
    rows = 80 * R
    bias_out = bout_ref[...].reshape(1, 384)
    group_out = lax.broadcasted_iota(jnp.int32, (R, 1, 8, 384), 2)

    def weight(i, b, e):
        return weights[i, 3 * b + e]

    def product(i, h0):
        taps = [inner[i, pl.ds(h0 + b, R)].reshape(rows, 768) for b in range(3)]
        main_w = jnp.concatenate(
            [
                jnp.concatenate(
                    [
                        jnp.concatenate([weight(i, b, 1), weight(i, b, 0)], axis=1),
                        jnp.concatenate([weight(i, b, 2), weight(i, b, 1)], axis=1),
                    ],
                    axis=0,
                )
                for b in range(3)
            ],
            axis=0,
        )
        main = jnp.dot(jnp.concatenate(taps, axis=1), main_w, preferred_element_type=F32)
        left = jnp.dot(
            jnp.concatenate([tap[:, 384:] for tap in taps], axis=1),
            jnp.concatenate([weight(i, b, 0) for b in range(3)], axis=0),
            preferred_element_type=F32,
        )
        right = jnp.dot(
            jnp.concatenate([tap[:, :384] for tap in taps], axis=1),
            jnp.concatenate([weight(i, b, 2) for b in range(3)], axis=0),
            preferred_element_type=F32,
        )
        return (main, left, right)

    def finish(f, h0, main, left, right):
        left = left.reshape(R, 10, 8, 384)
        last = pltpu.roll(left[:, 9:10].reshape(8 * R, 384), 1, 0).reshape(R, 1, 8, 384)
        last = jnp.where(group_out == 0, 0.0, last)
        left = jnp.concatenate([last, left[:, 0:9]], axis=1).reshape(rows, 384)
        right = right.reshape(R, 10, 8, 384)
        head = pltpu.roll(right[:, 0:1].reshape(8 * R, 384), 8 * R - 1, 0).reshape(R, 1, 8, 384)
        head = jnp.where(group_out == 7, 0.0, head)
        right = jnp.concatenate([right[:, 1:10], head], axis=1).reshape(rows, 384)
        halves = (main[:, :384] + left + bias_out, main[:, 384:] + right + bias_out)
        for r in range(R):
            for s in range(2):
                for col in range(10):
                    at = 80 * r + 8 * col
                    for lane in range(3):
                        stage[f, 3 * r + lane, pl.ds(2 * col + s, 8, stride=20), :] = halves[s][
                            at : at + 8, 128 * lane : 128 * lane + 128
                        ]
        for r in range(R):
            for lane in range(3):
                packed[f, h0 + r, :, 128 * lane : 128 * lane + 128] = stage[
                    f, 3 * r + lane
                ].astype(BF16)

    def store(f, h0):
        return pltpu.make_async_copy(
            packed.at[f, pl.ds(h0, R)], out_ref.at[f, pl.ds(h0, R)], store_sem.at[f]
        )

    at = (0, 768, 1152, 1536)

    def finish_both(h0):
        for f in range(2):
            finish(f, h0, *[total[f, :, at[n] : at[n + 1]] for n in range(3)])

    def out_step(step, carry):
        h0 = step * R
        finish_both(jnp.maximum(h0 - R, 0))
        m1 = product(1, h0)
        m2 = product(2, h0)
        m0 = product(0, h0)
        for n, (u, v, w) in enumerate(zip(m0, m1, m2)):
            total[0, :, at[n] : at[n + 1]] = u + (v + w)
            total[1, :, at[n] : at[n + 1]] = c * (v - w)
        for n, u in enumerate(product(3, h0)):
            total[1, :, at[n] : at[n + 1]] = total[1, :, at[n] : at[n + 1]] + u

        @pl.when(step > 0)
        def _():
            store(0, h0 - R).start()
            store(1, h0 - R).start()

        return carry

    lax.fori_loop(0, 10 // R, out_step, 0)
    finish_both(10 - R)
    for f in range(2):
        store(f, 10 - R).start()
    for f in range(2):
        pltpu.make_async_copy(packed.at[f], out_ref.at[f], store_sem.at[f]).wait()


def convolve(
    clip_lengths, received, dense_in, conv_in_bias, conv_out_weight, mixed, conv_out_bias,
    rows_per_step=5,
):
    R = rows_per_step
    return pl.pallas_call(
        functools.partial(conv_kernel, rows_per_step=R),
        out_shape=jax.ShapeDtypeStruct((2, 10, 160, 384), BF16),
        in_specs=[
            pl.BlockSpec(memory_space=pltpu.SMEM),
            pl.BlockSpec(memory_space=pl.ANY),
            pl.BlockSpec(memory_space=pl.ANY),
            pl.BlockSpec(memory_space=pltpu.VMEM),
            pl.BlockSpec(memory_space=pl.ANY),
            pl.BlockSpec(memory_space=pl.ANY),
            pl.BlockSpec(memory_space=pltpu.VMEM),
        ],
        out_specs=pl.BlockSpec(memory_space=pl.ANY),
        scratch_shapes=[
            pltpu.VMEM((3, 8, 80, 128), BF16),
            pltpu.VMEM((3, 640, 128), F32),
            pltpu.VMEM((6, 560, 128), BF16),
            pltpu.VMEM((768, 1536), BF16),
            pltpu.VMEM((4, 12, 80, 768), BF16),
            pltpu.VMEM((4, 9, 384, 384), BF16),
            pltpu.VMEM((2, 80 * R, 1536), F32),
            pltpu.VMEM((2, 3 * R, 160, 128), F32),
            pltpu.VMEM((2, 10, 160, 384), BF16),
            pltpu.SemaphoreType.DMA,
            pltpu.SemaphoreType.DMA((5,)),
            pltpu.SemaphoreType.DMA((2,)),
        ],
        compiler_params=pltpu.CompilerParams(vmem_limit_bytes=60 << 20),
    )(
        clip_lengths, received, dense_in, conv_in_bias,
        conv_out_weight.reshape(27, 384, 384), mixed, conv_out_bias,
    )


def head_kernel(
    clip_ref, hidden_ref, mod_ref, weight_ref, bias_ref, win_ref, wout_ref,
    recv_ref, dense_ref, mixed_ref,
    tokens, rhs, aux, grid, outgoing, win, dense_in, raw, mixed,
    load_sem, weight_sem, store_sem, send_sem, recv_sem,
):
    slab = lax.axis_index("tm")
    band = lax.axis_index("height")
    slabs = lax.axis_size("tm")
    bands = lax.axis_size("height")

    barrier = pltpu.get_barrier_semaphore()
    for d in range(3):
        for o in range(bands):
            if d or o:
                source = (lax.rem(slab + slabs - d, slabs), lax.rem(band + bands - o, bands))
                pl.semaphore_signal(barrier, inc=1, device_id=source, device_id_type=MESH)

    def load(n):
        return pltpu.make_async_copy(
            hidden_ref.at[pl.ds(pl.multiple_of(160 * n, 16), 160)], tokens.at[n], load_sem.at[n]
        )

    for n in range(5):
        load(n).start()
    win_copy = pltpu.make_async_copy(win_ref, win, weight_sem.at[3])
    win_copy.start()
    raw_copies = [
        pltpu.make_async_copy(wout_ref.at[pl.ds(9 * a, 9)], raw.at[a], weight_sem.at[a])
        for a in range(3)
    ]
    for cp in raw_copies:
        cp.start()

    weight = weight_ref[...].astype(F32)
    row_id = lax.broadcasted_iota(jnp.int32, (16, 5120), 0)
    extra = jnp.where(row_id == 0, 1.0, 0.0)
    for f in range(2):
        frame = 2 * slab + f
        end = jnp.int32(0)
        shift, scale = mod_ref[0, 0:1, :], mod_ref[1, 0:1, :]
        for clip in range(1, clip_ref.shape[0]):
            end = end + clip_ref[clip - 1]
            later = frame >= end
            shift = jnp.where(later, mod_ref[0, clip : clip + 1, :], shift)
            scale = jnp.where(later, mod_ref[1, clip : clip + 1, :], scale)
        rhs[64 * f : 64 * f + 64, :] = (weight * (1.0 + scale)).astype(BF16)
        rhs[128 + 64 * f : 192 + 64 * f, :] = weight_ref[...]
        coarse = shift.astype(BF16).astype(F32)
        extra = jnp.where(row_id == 2 * f + 1, coarse, extra)
        extra = jnp.where(row_id == 2 * f + 2, shift - coarse, extra)
    aux[...] = extra.astype(BF16)
    contract = (((1,), (1,)), ((), ()))
    sums = lax.dot_general(aux[...], rhs[...], contract, preferred_element_type=F32)
    lane = lax.broadcasted_iota(jnp.int32, (1, 128), 1)
    head_bias = bias_ref[...].reshape(1, 64)
    col_sum = sums[0:1, 0:128]
    offset = (
        jnp.where(lane < 64, sums[1:2, 128:] + sums[2:3, 128:], sums[3:4, 128:] + sums[4:5, 128:])
        + jnp.concatenate([head_bias, head_bias], axis=1)
    )

    zeros = jnp.zeros((8, 128), F32)
    for q in range(20):
        grid[56 * q : 56 * q + 8, :] = zeros
        grid[56 * q + 48 : 56 * q + 56, :] = zeros

    def head_step(n, carry):
        load(n).wait()
        raw = lax.dot_general(tokens[n], rhs[0:128, :], contract, preferred_element_type=F32)
        pivots, firsts, seconds = [], [], []
        for k in range(10):
            at = slice(16 * k, 16 * k + 16)
            pivot = tokens[n, at, 0:128].astype(F32)
            first = jnp.zeros((16, 128), F32)
            second = jnp.zeros((16, 128), F32)
            for tile in range(1, 40):
                v = tokens[n, at, 128 * tile : 128 * tile + 128].astype(F32) - pivot
                first = first + v
                second = second + v * v
            pivots.append(pivot)
            firsts.append(first)
            seconds.append(second)
        pivot = jnp.concatenate(pivots, axis=0)
        first = jnp.concatenate(firsts, axis=0)
        second = jnp.concatenate(seconds, axis=0)
        mean = jnp.sum(40.0 * pivot + first, axis=1, keepdims=True) / 5120.0
        gap = mean - pivot
        spread = second - 2.0 * gap * first + 40.0 * gap * gap
        scale = lax.rsqrt(jnp.sum(spread, axis=1, keepdims=True) / 5120.0 + 1e-06)
        value = scale * (raw - mean * col_sum) + offset
        for m in range(20):
            row = (4 * n + m // 5) * 56 + 8 + (m % 5) * 8
            grid[pl.ds(pl.multiple_of(row, 8), 8), :] = value[8 * m : 8 * m + 8]
        return carry

    lax.fori_loop(0, 5, head_step, 0)

    lane8 = lax.broadcasted_iota(jnp.int32, (8, 128), 1)
    for j in range(8):
        for pair in range(5):
            pieces = []
            for q in (2 * pair, 2 * pair + 1):
                at = 56 * q + 7 + 5 * j
                pieces.append(
                    jnp.where(lane8 < 64, grid[at : at + 8, :], grid[560 + at : 568 + at, :])
                )
            outgoing[j, 16 * pair : 16 * pair + 16, :] = jnp.concatenate(pieces, axis=0).astype(
                BF16
            )

    pl.semaphore_wait(barrier, 3 * bands - 1)
    copies = []
    for o in range(bands):
        to = lax.rem(band + o, bands)
        for d in range(3):
            target = recv_ref.at[2 - d, band]
            if d or o:
                cp = pltpu.make_async_remote_copy(
                    src_ref=outgoing.at[to],
                    dst_ref=target,
                    send_sem=send_sem.at[d, o],
                    recv_sem=recv_sem.at[d, o],
                    device_id=(lax.rem(slab + d, slabs), to),
                    device_id_type=MESH,
                )
            else:
                cp = pltpu.make_async_copy(outgoing.at[to], target, send_sem.at[d, o])
            cp.start()
            copies.append(cp)

    win_copy.wait()
    blank = jnp.zeros((16, 384), BF16)
    half = jnp.asarray(0.5, BF16)
    for a in range(3):
        for rr in range(4):
            for slot in range(4):
                for p in range(2):
                    for s in range(2):
                        b, e = rr - p, slot - s
                        ok = 0 <= b < 3 and 0 <= e < 3
                        row = a * 256 + rr * 64 + slot * 16
                        col = (2 * p + s) * 384
                        dense_in[row : row + 16, col : col + 384] = (
                            win[9 * a + 3 * b + e] * half if ok else blank
                        )
    dense_store = pltpu.make_async_copy(dense_in, dense_ref, store_sem.at[2])
    dense_store.start()

    second = 2 * slab + 1
    starts = second == 0
    end = jnp.int32(0)
    for clip in range(clip_ref.shape[0] - 1):
        end = end + clip_ref[clip]
        starts = jnp.logical_or(starts, second == end)
    for cp in raw_copies:
        cp.wait()

    def mix(k, carry):
        w0, w1, w2 = (raw[a, k].astype(F32) for a in range(3))
        outer = 0.5 * (w0 + w2)
        mid = 0.5 * w1
        mixed[0, k] = jnp.where(starts, w1, outer + mid).astype(BF16)
        mixed[1, k] = jnp.where(starts, w2, outer - mid).astype(BF16)
        return carry

    lax.fori_loop(0, 9, mix, 0)
    mixed_stores = [
        pltpu.make_async_copy(mixed.at[i], mixed_ref.at[i], store_sem.at[i]) for i in range(2)
    ]
    for cp in mixed_stores:
        cp.start()
    for cp in copies + mixed_stores + [dense_store]:
        cp.wait()


def head(
    clip_lengths, hidden, modulation, head_weight, head_bias, conv_in_weight, conv_out_weight
):
    return pl.pallas_call(
        head_kernel,
        out_shape=(
            jax.ShapeDtypeStruct((3, 8, 80, 128), BF16),
            jax.ShapeDtypeStruct((768, 1536), BF16),
            jax.ShapeDtypeStruct((2, 9, 384, 384), BF16),
        ),
        in_specs=[
            pl.BlockSpec(memory_space=pltpu.SMEM),
            pl.BlockSpec(memory_space=pl.ANY),
            pl.BlockSpec(memory_space=pltpu.VMEM),
            pl.BlockSpec(memory_space=pltpu.VMEM),
            pl.BlockSpec(memory_space=pltpu.VMEM),
            pl.BlockSpec(memory_space=pl.ANY),
            pl.BlockSpec(memory_space=pl.ANY),
        ],
        out_specs=[pl.BlockSpec(memory_space=pl.ANY)] * 3,
        scratch_shapes=[
            pltpu.VMEM((5, 160, 5120), BF16),
            pltpu.VMEM((256, 5120), BF16),
            pltpu.VMEM((16, 5120), BF16),
            pltpu.VMEM((1120, 128), F32),
            pltpu.VMEM((8, 80, 128), BF16),
            pltpu.VMEM((27, 16, 384), BF16),
            pltpu.VMEM((768, 1536), BF16),
            pltpu.VMEM((3, 9, 384, 384), BF16),
            pltpu.VMEM((2, 9, 384, 384), BF16),
            pltpu.SemaphoreType.DMA((5,)),
            pltpu.SemaphoreType.DMA((4,)),
            pltpu.SemaphoreType.DMA((3,)),
            pltpu.SemaphoreType.DMA((3, 8)),
            pltpu.SemaphoreType.DMA((3, 8)),
        ],
        compiler_params=pltpu.CompilerParams(
            collective_id=0, has_side_effects=True, vmem_limit_bytes=60 << 20
        ),
    )(
        clip_lengths,
        hidden.transpose(0, 2, 1, 3).reshape(800, 5120),
        modulation,
        head_weight.T,
        head_bias,
        conv_in_weight.reshape(27, 16, 384),
        conv_out_weight.reshape(27, 384, 384),
    )


def on_device(
    hidden, modulation, clip_lengths, head_weight, head_bias,
    conv_in_weight, conv_in_bias, conv_out_weight, conv_out_bias,
):
    received, dense_in, mixed = head(
        clip_lengths, hidden, modulation, head_weight, head_bias, conv_in_weight, conv_out_weight
    )
    return convolve(
        clip_lengths, received, dense_in, conv_in_bias, conv_out_weight, mixed, conv_out_bias
    )


def solution(mesh):
    return jax.shard_map(
        on_device,
        mesh=mesh,
        in_specs=(P("tm", None, "height", None), P(), P(), P(), P(), P(), P(), P(), P()),
        out_specs=P("tm", "height", None, None),
        check_vma=False,
    )
```

```python
import functools

import jax
import jax.numpy as jnp
from jax import lax
from jax.experimental import pallas as pl
from jax.experimental.pallas import tpu as pltpu
from jax.sharding import PartitionSpec as P

F32 = jnp.float32
BF16 = jnp.bfloat16
MESH = pl.DeviceIdType.MESH


def clip_start(clip_ref, frame):
    first = jnp.int32(0)
    end = jnp.int32(0)
    for clip in range(clip_ref.shape[0] - 1):
        end = end + clip_ref[clip]
        first = jnp.where(frame >= end, end, first)
    return first


def conv_kernel(
    clip_ref, recv_ref, dense_ref, bin_ref, wout_ref, mixed_ref, bout_ref, out_ref,
    received, spread, tokens, dense_in, inner, weights, total, stage, packed,
    recv_sem, load_sem, store_sem, *, rows_per_step,
):
    slab = lax.axis_index("tm")
    band = lax.axis_index("height")
    frame0 = 2 * slab

    recv_copy = pltpu.make_async_copy(recv_ref, received, recv_sem)
    recv_copy.start()
    dense_copy = pltpu.make_async_copy(dense_ref, dense_in, load_sem.at[4])
    dense_copy.start()
    sources = (
        wout_ref.at[pl.ds(0, 9)], mixed_ref.at[0], mixed_ref.at[1], wout_ref.at[pl.ds(18, 9)]
    )
    loads = [
        pltpu.make_async_copy(sources[i], weights.at[i], load_sem.at[i]) for i in range(4)
    ]

    lane_in = lax.broadcasted_iota(jnp.int32, (128, 256), 0)
    lane_out = lax.broadcasted_iota(jnp.int32, (128, 256), 1)
    wanted = (
        (lane_out // 128) * 64
        + ((lane_out // 64) % 2) * 32
        + ((lane_out // 16 + 1) % 2) * 16
        + lane_out % 16
    )
    spreader = jnp.where(lane_in == wanted, 1.0, 0.0).astype(BF16)
    slot_id = (lax.broadcasted_iota(jnp.int32, (7, 10, 8, 128), 3) // 16) % 4
    group_id = lax.broadcasted_iota(jnp.int32, (7, 1, 8, 128), 2)
    recv_copy.wait()
    for back in range(3):
        for src in range(8):
            block = received[back, src].astype(F32)
            for col in range(10):
                spread[back, pl.ds(8 * col + src, 8, stride=80), :] = block[8 * col : 8 * col + 8]
    for back in range(3):
        both = jnp.dot(spread[back, 0:560, :].astype(BF16), spreader, preferred_element_type=F32)
        for f in range(2):
            here = both[:, 128 * f : 128 * f + 128].reshape(7, 10, 8, 128)
            last = pltpu.roll(here[:, 9:10].reshape(56, 128), 1, 0).reshape(7, 1, 8, 128)
            last = jnp.where(group_id == 0, 0.0, last)
            head = pltpu.roll(here[:, 0:1].reshape(56, 128), 55, 0).reshape(7, 1, 8, 128)
            head = jnp.where(group_id == 7, 0.0, head)
            before = jnp.concatenate([last, here[:, 0:9]], axis=1)
            after = jnp.concatenate([here[:, 1:10], head], axis=1)
            mixed_slots = jnp.where(slot_id == 0, before, jnp.where(slot_id == 3, after, here))
            tokens[2 * back + f] = mixed_slots.reshape(560, 128).astype(BF16)

    keep = []
    for g in range(4):
        first = clip_start(clip_ref, frame0 - 2 + g)
        keep.append([frame0 - 4 + g + a >= first for a in range(3)])
    first0 = clip_start(clip_ref, frame0)
    use0 = frame0 - 2 >= first0
    use1 = frame0 - 1 >= first0
    joined = frame0 >= clip_start(clip_ref, frame0 + 1)
    c = jnp.where(joined, 1.0, 0.0).astype(F32)
    c16 = c.astype(BF16)
    halved = jnp.where(joined, 0.5, 1.0).astype(F32)
    paired = jnp.where(joined, 0.5, 0.0).astype(F32)
    bias_in = 0.5 * bin_ref[...].reshape(1, 384)
    bias_in = jnp.concatenate([bias_in, bias_in], axis=1)
    dense_copy.wait()
    for i in (1, 2, 0, 3):
        loads[i].start()

    def in_step(step, carry):
        i0 = 2 * step
        for p in range(2):
            x = []
            for g in range(4):
                parts = []
                for a in range(3):
                    lo = tokens[g + a, pl.ds(pl.multiple_of(i0 * 80, 16), 160), :]
                    hi = tokens[g + a, pl.ds(pl.multiple_of(i0 * 80 + 80, 16), 160), :]
                    both = jnp.concatenate([lo, hi], axis=1)
                    if a < 2:
                        both = jnp.where(keep[g][a], both, jnp.zeros_like(both))
                    parts.append(both)
                v = jnp.dot(
                    jnp.concatenate(parts, axis=1),
                    dense_in[:, 768 * p : 768 * p + 768],
                    preferred_element_type=F32,
                )
                v = v + bias_in
                x.append((v + v * jnp.tanh(v)).astype(BF16))
            zero = jnp.zeros_like(x[0])
            x0 = jnp.where(use0, x[0], zero)
            x1 = jnp.where(use1, x[1], zero)
            x2, x3 = x[2], x[3]
            x1c, x2c = c16 * x1, c16 * x2
            sums = (x0 - x2c, x1 + x2c, x2 - x1c, x3 - x1c)
            for r in range(2):
                for i in range(4):
                    inner[i, 4 * step + 2 * r + p] = sums[i][80 * r : 80 * r + 80]
        return carry

    lax.fori_loop(0, 3, in_step, 0)

    @pl.when(band == 0)
    def _():
        inner[:, 0] = jnp.zeros((4, 80, 768), BF16)

    @pl.when(band == 7)
    def _():
        inner[:, 11] = jnp.zeros((4, 80, 768), BF16)

    for cp in loads:
        cp.wait()

    R = rows_per_step
    rows = 80 * R
    bias_out = bout_ref[...].reshape(1, 384)
    group_out = lax.broadcasted_iota(jnp.int32, (R, 1, 8, 384), 2)

    def weight(i, b, e):
        return weights[i, 3 * b + e]

    def product(i, h0):
        taps = [inner[i, pl.ds(h0 + b, R)].reshape(rows, 768) for b in range(3)]
        main_w = jnp.concatenate(
            [
                jnp.concatenate(
                    [
                        jnp.concatenate([weight(i, b, 1), weight(i, b, 0)], axis=1),
                        jnp.concatenate([weight(i, b, 2), weight(i, b, 1)], axis=1),
                    ],
                    axis=0,
                )
                for b in range(3)
            ],
            axis=0,
        )
        main = jnp.dot(jnp.concatenate(taps, axis=1), main_w, preferred_element_type=F32)
        left = jnp.dot(
            jnp.concatenate([tap[:, 384:] for tap in taps], axis=1),
            jnp.concatenate([weight(i, b, 0) for b in range(3)], axis=0),
            preferred_element_type=F32,
        )
        right = jnp.dot(
            jnp.concatenate([tap[:, :384] for tap in taps], axis=1),
            jnp.concatenate([weight(i, b, 2) for b in range(3)], axis=0),
            preferred_element_type=F32,
        )
        return (main, left, right)

    def finish(f, h0, main, left, right):
        left = left.reshape(R, 10, 8, 384)
        last = pltpu.roll(left[:, 9:10].reshape(8 * R, 384), 1, 0).reshape(R, 1, 8, 384)
        last = jnp.where(group_out == 0, 0.0, last)
        left = jnp.concatenate([last, left[:, 0:9]], axis=1).reshape(rows, 384)
        right = right.reshape(R, 10, 8, 384)
        head = pltpu.roll(right[:, 0:1].reshape(8 * R, 384), 8 * R - 1, 0).reshape(R, 1, 8, 384)
        head = jnp.where(group_out == 7, 0.0, head)
        right = jnp.concatenate([right[:, 1:10], head], axis=1).reshape(rows, 384)
        halves = (main[:, :384] + left + bias_out, main[:, 384:] + right + bias_out)
        for r in range(R):
            for s in range(2):
                for col in range(10):
                    at = 80 * r + 8 * col
                    for lane in range(3):
                        stage[f, 3 * r + lane, pl.ds(2 * col + s, 8, stride=20), :] = halves[s][
                            at : at + 8, 128 * lane : 128 * lane + 128
                        ]
        for r in range(R):
            for lane in range(3):
                packed[f, h0 + r, :, 128 * lane : 128 * lane + 128] = stage[
                    f, 3 * r + lane
                ].astype(BF16)

    def store(f, h0):
        return pltpu.make_async_copy(
            packed.at[f, pl.ds(h0, R)], out_ref.at[f, pl.ds(h0, R)], store_sem.at[f]
        )

    at = (0, 768, 1152, 1536)

    def finish_both(h0):
        for f in range(2):
            finish(f, h0, *[total[f, :, at[n] : at[n + 1]] for n in range(3)])

    def out_step(step, carry):
        h0 = step * R
        finish_both(jnp.maximum(h0 - R, 0))
        m1 = product(1, h0)
        m2 = product(2, h0)
        m0 = product(0, h0)
        for n, (u, v, w) in enumerate(zip(m0, m1, m2)):
            total[0, :, at[n] : at[n + 1]] = u + halved * (v + w)
            total[1, :, at[n] : at[n + 1]] = paired * (v - w)
        for n, u in enumerate(product(3, h0)):
            total[1, :, at[n] : at[n + 1]] = total[1, :, at[n] : at[n + 1]] + u

        @pl.when(step > 0)
        def _():
            store(0, h0 - R).start()
            store(1, h0 - R).start()

        return carry

    lax.fori_loop(0, 10 // R, out_step, 0)
    finish_both(10 - R)
    for f in range(2):
        store(f, 10 - R).start()
    for f in range(2):
        pltpu.make_async_copy(packed.at[f], out_ref.at[f], store_sem.at[f]).wait()


def convolve(
    clip_lengths, received, dense_in, conv_in_bias, conv_out_weight, mixed, conv_out_bias,
    rows_per_step=5,
):
    R = rows_per_step
    return pl.pallas_call(
        functools.partial(conv_kernel, rows_per_step=R),
        out_shape=jax.ShapeDtypeStruct((2, 10, 160, 384), BF16),
        in_specs=[
            pl.BlockSpec(memory_space=pltpu.SMEM),
            pl.BlockSpec(memory_space=pl.ANY),
            pl.BlockSpec(memory_space=pl.ANY),
            pl.BlockSpec(memory_space=pltpu.VMEM),
            pl.BlockSpec(memory_space=pl.ANY),
            pl.BlockSpec(memory_space=pl.ANY),
            pl.BlockSpec(memory_space=pltpu.VMEM),
        ],
        out_specs=pl.BlockSpec(memory_space=pl.ANY),
        scratch_shapes=[
            pltpu.VMEM((3, 8, 80, 128), BF16),
            pltpu.VMEM((3, 640, 128), F32),
            pltpu.VMEM((6, 560, 128), BF16),
            pltpu.VMEM((768, 1536), BF16),
            pltpu.VMEM((4, 12, 80, 768), BF16),
            pltpu.VMEM((4, 9, 384, 384), BF16),
            pltpu.VMEM((2, 80 * R, 1536), F32),
            pltpu.VMEM((2, 3 * R, 160, 128), F32),
            pltpu.VMEM((2, 10, 160, 384), BF16),
            pltpu.SemaphoreType.DMA,
            pltpu.SemaphoreType.DMA((5,)),
            pltpu.SemaphoreType.DMA((2,)),
        ],
        compiler_params=pltpu.CompilerParams(vmem_limit_bytes=60 << 20),
    )(
        clip_lengths, received, dense_in, conv_in_bias,
        conv_out_weight.reshape(27, 384, 384), mixed, conv_out_bias,
    )


def head_kernel(
    clip_ref, hidden_ref, mod_ref, weight_ref, bias_ref, win_ref, wout_ref,
    recv_ref, dense_ref, mixed_ref,
    tokens, mod, weight, rhs, aux, raw, moments, grid, outgoing, win, dense_in, taps, mixed,
    load_sem, small_sem, tap_sem, store_sem, send_sem, recv_sem,
):
    slab = lax.axis_index("tm")
    band = lax.axis_index("height")
    slabs = lax.axis_size("tm")
    bands = lax.axis_size("height")
    small = [
        pltpu.make_async_copy(weight_ref, weight, small_sem.at[0]),
        pltpu.make_async_copy(mod_ref, mod, small_sem.at[1]),
    ]
    for cp in small:
        cp.start()

    def load(n):
        return pltpu.make_async_copy(
            hidden_ref.at[pl.ds(pl.multiple_of(160 * n, 16), 160)], tokens.at[n], load_sem.at[n]
        )

    for n in range(1):
        load(n).start()
    win_copy = pltpu.make_async_copy(win_ref, win, small_sem.at[2])
    win_copy.start()

    barrier = pltpu.get_barrier_semaphore()
    for d in range(3):

        @pl.when(slab >= d)
        def _():
            for o in range(bands):
                if d or o:
                    source = (slab - d, lax.rem(band + bands - o, bands))
                    pl.semaphore_signal(barrier, inc=1, device_id=source, device_id_type=MESH)

    def load_taps(k):
        at = pl.ds(3 * k, 3)
        return pltpu.make_async_copy(wout_ref.at[:, at], taps.at[:, at], tap_sem.at[k])

    for cp in small:
        cp.wait()
    for n in range(1, 3):
        load(n).start()
    weights = weight[...].astype(F32)
    row_id = lax.broadcasted_iota(jnp.int32, (16, 5120), 0)
    extra = jnp.where(row_id == 0, 1.0, 0.0)
    scaled = []
    for f in range(2):
        frame = 2 * slab + f
        end = jnp.int32(0)
        shift, scale = mod[0, 0:1, :], mod[1, 0:1, :]
        for clip in range(1, clip_ref.shape[0]):
            end = end + clip_ref[clip - 1]
            later = frame >= end
            shift = jnp.where(later, mod[0, clip : clip + 1, :], shift)
            scale = jnp.where(later, mod[1, clip : clip + 1, :], scale)
        scaled.append((weights * (1.0 + scale)).astype(BF16))
        coarse = shift.astype(BF16).astype(F32)
        extra = jnp.where(row_id == 2 * f + 1, coarse, extra)
        extra = jnp.where(row_id == 2 * f + 2, shift - coarse, extra)
    aux[...] = extra.astype(BF16)
    contract = (((1,), (1,)), ((), ()))
    scaled = jnp.concatenate(scaled, axis=0)
    ones = jnp.ones((128, 128), BF16)
    for k in range(40):
        rhs[128 * k : 128 * k + 128, 0:128] = scaled[:, 128 * k : 128 * k + 128].T
        rhs[128 * k : 128 * k + 128, 128:256] = ones
    col_sum = jnp.dot(aux[...], rhs[...], preferred_element_type=F32)[0:1, 0:128]
    sums = lax.dot_general(aux[...], weight[...], contract, preferred_element_type=F32)
    head_bias = bias_ref[...].reshape(1, 64)
    offset = jnp.concatenate(
        [sums[1:2] + sums[2:3] + head_bias, sums[3:4] + sums[4:5] + head_bias], axis=1
    )

    grid[...] = jnp.zeros_like(grid)
    lane8 = lax.broadcasted_iota(jnp.int32, (8, 128), 1)

    def settle(n):
        pivot, second = moments[0], moments[1]
        mean = raw[:, 128:256] * (1.0 / 5120.0)
        gap = mean - pivot
        var = jnp.sum(second, axis=1, keepdims=True) * (1.0 / 5120.0) - gap * gap
        value = lax.rsqrt(var + 1e-06) * (raw[:, 0:128] - mean * col_sum) + offset
        for m in range(20):
            q = 4 * n + m // 5
            own = (lane8 < 64) == (q < 10)
            row = lax.rem(q, 10) * 56 + 8 + (m % 5) * 8
            at = pl.ds(pl.multiple_of(row, 8), 8)
            grid[at, :] = jnp.where(own, value[8 * m : 8 * m + 8], grid[at, :])

    def head_step(n, carry):
        load(n).wait()

        @pl.when(n < 2)
        def _():
            load(n + 3).start()

        settle(jnp.maximum(n - 1, 0))
        sample = jnp.sum(tokens[n, :, 0:128].astype(F32), axis=1, keepdims=True) * (1.0 / 128.0)
        pivot = jnp.broadcast_to(sample, (160, 128))
        moments[0] = pivot
        for k in range(10):
            at = slice(16 * k, 16 * k + 16)
            second = jnp.zeros((16, 128), F32)
            for tile in range(40):
                v = tokens[n, at, 128 * tile : 128 * tile + 128].astype(F32) - pivot[at]
                second = second + v * v
            moments[1, at] = second
        raw[...] = jnp.dot(tokens[n], rhs[...], preferred_element_type=F32)
        return carry

    lax.fori_loop(0, 5, head_step, 0)
    for k in range(2):
        load_taps(k).start()
    settle(4)

    for j in range(8):
        for pair in range(5):
            pieces = []
            for q in (2 * pair, 2 * pair + 1):
                at = 56 * q + 7 + 5 * j
                pieces.append(grid[at : at + 8, :])
            outgoing[j, 16 * pair : 16 * pair + 16, :] = jnp.concatenate(pieces, axis=0).astype(
                BF16
            )

    def send(d, o):
        to = lax.rem(band + o, bands)
        return pltpu.make_async_remote_copy(
            src_ref=outgoing.at[to],
            dst_ref=recv_ref.at[2 - d, band],
            send_sem=send_sem.at[d, o],
            recv_sem=recv_sem.at[d, o],
            device_id=(slab + d, to),
            device_id_type=MESH,
        )

    pl.semaphore_wait(
        barrier,
        bands * jnp.minimum(slabs - slab, 3) - 1,
    )
    for d in (2, 1, 0):

        @pl.when(slab + d < slabs)
        def _():
            for o in range(1, bands + 1):
                if d or o < bands:
                    send(d, o % bands).start()

    own_copy = pltpu.make_async_copy(outgoing.at[band], recv_ref.at[2, band], small_sem.at[0])
    own_copy.start()

    win_copy.wait()
    blank = jnp.zeros((16, 384), BF16)
    half = jnp.asarray(0.5, BF16)
    for a in range(3):
        for rr in range(4):
            for slot in range(4):
                for p in range(2):
                    for s in range(2):
                        b, e = rr - p, slot - s
                        ok = 0 <= b < 3 and 0 <= e < 3
                        row = a * 256 + rr * 64 + slot * 16
                        col = (2 * p + s) * 384
                        dense_in[row : row + 16, col : col + 384] = (
                            win[9 * a + 3 * b + e] * half if ok else blank
                        )
    dense_store = pltpu.make_async_copy(dense_in, dense_ref, store_sem.at[3])
    dense_store.start()

    second_frame = 2 * slab + 1
    starts = second_frame == 0
    end = jnp.int32(0)
    for clip in range(clip_ref.shape[0] - 1):
        end = end + clip_ref[clip]
        starts = jnp.logical_or(starts, second_frame == end)

    def store_mixed(k):
        at = pl.ds(3 * k, 3)
        return pltpu.make_async_copy(mixed.at[:, at], mixed_ref.at[:, at], store_sem.at[k])

    def mix(k, carry):
        w0, w1, w2 = (taps[a, k].astype(F32) for a in range(3))
        outer = w0 + w2
        mixed[0, k] = jnp.where(starts, taps[1, k], (outer + w1).astype(BF16))
        mixed[1, k] = jnp.where(starts, taps[2, k], (outer - w1).astype(BF16))
        return carry

    for k in range(3):
        load_taps(k).wait()
        if k == 0:
            load_taps(2).start()
        lax.fori_loop(3 * k, 3 * k + 3, mix, 0)
        store_mixed(k).start()

    own_copy.wait()
    for d in range(3):

        @pl.when(slab + d < slabs)
        def _():
            for o in range(bands):
                if d or o:
                    send(d, o).wait_send()

        @pl.when(slab >= d)
        def _():
            for o in range(bands):
                if d or o:
                    send(d, o).wait_recv()

    dense_store.wait()
    for k in range(3):
        store_mixed(k).wait()


def head(
    clip_lengths, hidden, modulation, head_weight, head_bias, conv_in_weight, conv_out_weight
):
    return pl.pallas_call(
        head_kernel,
        out_shape=(
            jax.ShapeDtypeStruct((3, 8, 80, 128), BF16),
            jax.ShapeDtypeStruct((768, 1536), BF16),
            jax.ShapeDtypeStruct((2, 9, 384, 384), BF16),
        ),
        in_specs=[
            pl.BlockSpec(memory_space=pltpu.SMEM),
            pl.BlockSpec(memory_space=pl.ANY),
            pl.BlockSpec(memory_space=pl.ANY),
            pl.BlockSpec(memory_space=pl.ANY),
            pl.BlockSpec(memory_space=pltpu.VMEM),
            pl.BlockSpec(memory_space=pl.ANY),
            pl.BlockSpec(memory_space=pl.ANY),
        ],
        out_specs=[pl.BlockSpec(memory_space=pl.ANY)] * 3,
        scratch_shapes=[
            pltpu.VMEM((5, 160, 5120), BF16),
            pltpu.VMEM((2, 4, 5120), F32),
            pltpu.VMEM((64, 5120), BF16),
            pltpu.VMEM((5120, 256), BF16),
            pltpu.VMEM((16, 5120), BF16),
            pltpu.VMEM((160, 256), F32),
            pltpu.VMEM((2, 160, 128), F32),
            pltpu.VMEM((560, 128), F32),
            pltpu.VMEM((8, 80, 128), BF16),
            pltpu.VMEM((27, 16, 384), BF16),
            pltpu.VMEM((768, 1536), BF16),
            pltpu.VMEM((3, 9, 384, 384), BF16),
            pltpu.VMEM((2, 9, 384, 384), BF16),
            pltpu.SemaphoreType.DMA((5,)),
            pltpu.SemaphoreType.DMA((3,)),
            pltpu.SemaphoreType.DMA((3,)),
            pltpu.SemaphoreType.DMA((4,)),
            pltpu.SemaphoreType.DMA((3, 8)),
            pltpu.SemaphoreType.DMA((3, 8)),
        ],
        compiler_params=pltpu.CompilerParams(
            collective_id=0, has_side_effects=True, vmem_limit_bytes=60 << 20
        ),
    )(
        clip_lengths,
        hidden.transpose(0, 2, 1, 3).reshape(800, 5120),
        modulation,
        head_weight.T,
        head_bias,
        conv_in_weight.reshape(27, 16, 384),
        conv_out_weight.reshape(3, 9, 384, 384),
    )


def on_device(
    hidden, modulation, clip_lengths, head_weight, head_bias,
    conv_in_weight, conv_in_bias, conv_out_weight, conv_out_bias,
):
    received, dense_in, mixed = head(
        clip_lengths, hidden, modulation, head_weight, head_bias, conv_in_weight, conv_out_weight
    )
    return convolve(
        clip_lengths, received, dense_in, conv_in_bias, conv_out_weight, mixed, conv_out_bias
    )


def solution(mesh):
    return jax.shard_map(
        on_device,
        mesh=mesh,
        in_specs=(P("tm", None, "height", None), P(), P(), P(), P(), P(), P(), P(), P()),
        out_specs=P("tm", "height", None, None),
        check_vma=False,
    )
```

```python
import functools

import jax
import jax.numpy as jnp
from jax import lax
from jax.experimental import pallas as pl
from jax.experimental.pallas import tpu as pltpu
from jax.sharding import PartitionSpec as P

F32 = jnp.float32
BF16 = jnp.bfloat16
MESH = pl.DeviceIdType.MESH


def clip_start(clip_ref, frame):
    first = jnp.int32(0)
    end = jnp.int32(0)
    for clip in range(clip_ref.shape[0] - 1):
        end = end + clip_ref[clip]
        first = jnp.where(frame >= end, end, first)
    return first


def conv_kernel(
    clip_ref, recv_ref, dense_ref, bin_ref, wout_ref, mixed_ref, bout_ref, out_ref,
    received, spread, tokens, dense_in, inner, weights, total, stage, packed,
    recv_sem, load_sem, store_sem, *, rows_per_step,
):
    slab = lax.axis_index("tm")
    band = lax.axis_index("height")
    frame0 = 2 * slab

    recv_copy = pltpu.make_async_copy(recv_ref, received, recv_sem)
    recv_copy.start()
    dense_copy = pltpu.make_async_copy(dense_ref, dense_in, load_sem.at[4])
    dense_copy.start()
    sources = (
        wout_ref.at[pl.ds(0, 9)], mixed_ref.at[0], mixed_ref.at[1], wout_ref.at[pl.ds(18, 9)]
    )
    loads = [
        pltpu.make_async_copy(sources[i], weights.at[i], load_sem.at[i]) for i in range(4)
    ]

    lane_in = lax.broadcasted_iota(jnp.int32, (128, 256), 0)
    lane_out = lax.broadcasted_iota(jnp.int32, (128, 256), 1)
    wanted = (
        (lane_out // 128) * 64
        + ((lane_out // 64) % 2) * 32
        + ((lane_out // 16 + 1) % 2) * 16
        + lane_out % 16
    )
    spreader = jnp.where(lane_in == wanted, 1.0, 0.0).astype(BF16)
    slot_id = (lax.broadcasted_iota(jnp.int32, (7, 10, 8, 128), 3) // 16) % 4
    group_id = lax.broadcasted_iota(jnp.int32, (7, 1, 8, 128), 2)
    recv_copy.wait()
    for back in range(3):
        for src in range(8):
            block = received[back, src].astype(F32)
            for col in range(10):
                spread[back, pl.ds(8 * col + src, 8, stride=80), :] = block[8 * col : 8 * col + 8]
    for back in range(3):
        both = jnp.dot(spread[back, 0:560, :].astype(BF16), spreader, preferred_element_type=F32)
        for f in range(2):
            here = both[:, 128 * f : 128 * f + 128].reshape(7, 10, 8, 128)
            last = pltpu.roll(here[:, 9:10].reshape(56, 128), 1, 0).reshape(7, 1, 8, 128)
            last = jnp.where(group_id == 0, 0.0, last)
            head = pltpu.roll(here[:, 0:1].reshape(56, 128), 55, 0).reshape(7, 1, 8, 128)
            head = jnp.where(group_id == 7, 0.0, head)
            before = jnp.concatenate([last, here[:, 0:9]], axis=1)
            after = jnp.concatenate([here[:, 1:10], head], axis=1)
            mixed_slots = jnp.where(slot_id == 0, before, jnp.where(slot_id == 3, after, here))
            tokens[2 * back + f] = mixed_slots.reshape(560, 128).astype(BF16)

    keep = []
    for g in range(4):
        first = clip_start(clip_ref, frame0 - 2 + g)
        keep.append([frame0 - 4 + g + a >= first for a in range(3)])
    first0 = clip_start(clip_ref, frame0)
    use0 = frame0 - 2 >= first0
    use1 = frame0 - 1 >= first0
    joined = frame0 >= clip_start(clip_ref, frame0 + 1)
    c = jnp.where(joined, 1.0, 0.0).astype(F32)
    c16 = c.astype(BF16)
    halved = jnp.where(joined, 0.5, 1.0).astype(F32)
    paired = jnp.where(joined, 0.5, 0.0).astype(F32)
    bias_in = 0.5 * bin_ref[...].reshape(1, 384)
    bias_in = jnp.concatenate([bias_in, bias_in], axis=1)
    dense_copy.wait()
    for i in (1, 2, 0, 3):
        loads[i].start()

    def in_step(step):
        i0 = 2 * step
        for p in range(2):
            x = []
            for g in range(4):
                parts = []
                for a in range(3):
                    lo = tokens[g + a, pl.ds(i0 * 80, 160), :]
                    hi = tokens[g + a, pl.ds(i0 * 80 + 80, 160), :]
                    both = jnp.concatenate([lo, hi], axis=1)
                    if a < 2:
                        both = jnp.where(keep[g][a], both, jnp.zeros_like(both))
                    parts.append(both)
                v = jnp.dot(
                    jnp.concatenate(parts, axis=1),
                    dense_in[:, 768 * p : 768 * p + 768],
                    preferred_element_type=F32,
                )
                v = v + bias_in
                x.append((v + v * jnp.tanh(v)).astype(BF16))
            zero = jnp.zeros_like(x[0])
            x0 = jnp.where(use0, x[0], zero)
            x1 = jnp.where(use1, x[1], zero)
            x2, x3 = x[2], x[3]
            x1c, x2c = c16 * x1, c16 * x2
            sums = (x0 - x2c, x1 + x2c, x2 - x1c, x3 - x1c)
            for r in range(2):
                for i in range(4):
                    inner[i, 4 * step + 2 * r + p] = sums[i][80 * r : 80 * r + 80]

    for step in range(3):
        in_step(step)

    @pl.when(band == 0)
    def _():
        inner[:, 0] = jnp.zeros((4, 80, 768), BF16)

    @pl.when(band == 7)
    def _():
        inner[:, 11] = jnp.zeros((4, 80, 768), BF16)

    for cp in loads:
        cp.wait()

    R = rows_per_step
    rows = 80 * R
    bias_out = bout_ref[...].reshape(1, 384)
    group_out = lax.broadcasted_iota(jnp.int32, (R, 1, 8, 384), 2)

    def weight(i, b, e):
        return weights[i, 3 * b + e]

    def product(i, h0):
        taps = [inner[i, pl.ds(h0 + b, R)].reshape(rows, 768) for b in range(3)]
        main_w = jnp.concatenate(
            [
                jnp.concatenate(
                    [
                        jnp.concatenate([weight(i, b, 1), weight(i, b, 0)], axis=1),
                        jnp.concatenate([weight(i, b, 2), weight(i, b, 1)], axis=1),
                    ],
                    axis=0,
                )
                for b in range(3)
            ],
            axis=0,
        )
        main = jnp.dot(jnp.concatenate(taps, axis=1), main_w, preferred_element_type=F32)
        left = jnp.dot(
            jnp.concatenate([tap[:, 384:] for tap in taps], axis=1),
            jnp.concatenate([weight(i, b, 0) for b in range(3)], axis=0),
            preferred_element_type=F32,
        )
        right = jnp.dot(
            jnp.concatenate([tap[:, :384] for tap in taps], axis=1),
            jnp.concatenate([weight(i, b, 2) for b in range(3)], axis=0),
            preferred_element_type=F32,
        )
        return (main, left, right)

    def finish(f, h0, main, left, right):
        left = left.reshape(R, 10, 8, 384)
        last = pltpu.roll(left[:, 9:10].reshape(8 * R, 384), 1, 0).reshape(R, 1, 8, 384)
        last = jnp.where(group_out == 0, 0.0, last)
        left = jnp.concatenate([last, left[:, 0:9]], axis=1).reshape(rows, 384)
        right = right.reshape(R, 10, 8, 384)
        head = pltpu.roll(right[:, 0:1].reshape(8 * R, 384), 8 * R - 1, 0).reshape(R, 1, 8, 384)
        head = jnp.where(group_out == 7, 0.0, head)
        right = jnp.concatenate([right[:, 1:10], head], axis=1).reshape(rows, 384)
        halves = (main[:, :384] + left + bias_out, main[:, 384:] + right + bias_out)
        for r in range(R):
            for s in range(2):
                for col in range(10):
                    at = 80 * r + 8 * col
                    for lane in range(3):
                        stage[f, 3 * r + lane, pl.ds(2 * col + s, 8, stride=20), :] = halves[s][
                            at : at + 8, 128 * lane : 128 * lane + 128
                        ]
        for r in range(R):
            for lane in range(3):
                packed[f, h0 + r, :, 128 * lane : 128 * lane + 128] = stage[
                    f, 3 * r + lane
                ].astype(BF16)

    def store(f, h0):
        return pltpu.make_async_copy(
            packed.at[f, pl.ds(h0, R)], out_ref.at[f, pl.ds(h0, R)], store_sem.at[f]
        )

    at = (0, 768, 1152, 1536)

    def finish_one(f, h0):
        finish(f, h0, *[total[f, :, at[n] : at[n + 1]] for n in range(3)])

    for h0 in range(0, 10, R):
        if h0 > 0:
            for f in range(2):
                finish_one(f, h0 - R)
        m1 = product(1, h0)
        m2 = product(2, h0)
        m0 = product(0, h0)
        for n, (u, v, w) in enumerate(zip(m0, m1, m2)):
            total[0, :, at[n] : at[n + 1]] = u + halved * (v + w)
            total[1, :, at[n] : at[n + 1]] = paired * (v - w)
        if h0 + R == 10:
            finish_one(0, h0)
        for n, u in enumerate(product(3, h0)):
            total[1, :, at[n] : at[n + 1]] = total[1, :, at[n] : at[n + 1]] + u
        if h0 > 0:
            for f in range(2):
                store(f, h0 - R).start()
    store(0, 10 - R).start()
    finish_one(1, 10 - R)
    store(1, 10 - R).start()
    for f in range(2):
        pltpu.make_async_copy(packed.at[f], out_ref.at[f], store_sem.at[f]).wait()


def convolve(
    clip_lengths, received, dense_in, conv_in_bias, conv_out_weight, mixed, conv_out_bias,
    rows_per_step=2,
):
    R = rows_per_step
    return pl.pallas_call(
        functools.partial(conv_kernel, rows_per_step=R),
        out_shape=jax.ShapeDtypeStruct((2, 10, 160, 384), BF16),
        in_specs=[
            pl.BlockSpec(memory_space=pltpu.SMEM),
            pl.BlockSpec(memory_space=pl.ANY),
            pl.BlockSpec(memory_space=pl.ANY),
            pl.BlockSpec(memory_space=pltpu.VMEM),
            pl.BlockSpec(memory_space=pl.ANY),
            pl.BlockSpec(memory_space=pl.ANY),
            pl.BlockSpec(memory_space=pltpu.VMEM),
        ],
        out_specs=pl.BlockSpec(memory_space=pl.ANY),
        scratch_shapes=[
            pltpu.VMEM((3, 8, 80, 128), BF16),
            pltpu.VMEM((3, 640, 128), F32),
            pltpu.VMEM((6, 560, 128), BF16),
            pltpu.VMEM((768, 1536), BF16),
            pltpu.VMEM((4, 12, 80, 768), BF16),
            pltpu.VMEM((4, 9, 384, 384), BF16),
            pltpu.VMEM((2, 80 * R, 1536), F32),
            pltpu.VMEM((2, 3 * R, 160, 128), F32),
            pltpu.VMEM((2, 10, 160, 384), BF16),
            pltpu.SemaphoreType.DMA,
            pltpu.SemaphoreType.DMA((5,)),
            pltpu.SemaphoreType.DMA((2,)),
        ],
        compiler_params=pltpu.CompilerParams(vmem_limit_bytes=60 << 20),
    )(
        clip_lengths, received, dense_in, conv_in_bias,
        conv_out_weight.reshape(27, 384, 384), mixed, conv_out_bias,
    )


def head_kernel(
    clip_ref, hidden_ref, mod_ref, weight_ref, bias_ref, win_ref, wout_ref,
    recv_ref, dense_ref, mixed_ref,
    tokens, mod, weight, rhs, aux, raw, moments, grid, outgoing, win, dense_in, taps, mixed,
    load_sem, small_sem, tap_sem, store_sem, send_sem, recv_sem,
):
    slab = lax.axis_index("tm")
    band = lax.axis_index("height")
    slabs = lax.axis_size("tm")
    bands = lax.axis_size("height")
    small = [
        pltpu.make_async_copy(weight_ref, weight, small_sem.at[0]),
        pltpu.make_async_copy(mod_ref, mod, small_sem.at[1]),
    ]
    for cp in small:
        cp.start()

    def load(n):
        return pltpu.make_async_copy(
            hidden_ref.at[pl.ds(pl.multiple_of(160 * n, 16), 160)], tokens.at[n], load_sem.at[n]
        )

    for n in range(1):
        load(n).start()
    win_copy = pltpu.make_async_copy(win_ref, win, small_sem.at[2])
    win_copy.start()

    barrier = pltpu.get_barrier_semaphore()
    for d in range(3):

        @pl.when(slab >= d)
        def _():
            for o in range(bands):
                if d or o:
                    source = (slab - d, lax.rem(band + bands - o, bands))
                    pl.semaphore_signal(barrier, inc=1, device_id=source, device_id_type=MESH)

    def load_taps(k):
        at = pl.ds(3 * k, 3)
        return pltpu.make_async_copy(wout_ref.at[:, at], taps.at[:, at], tap_sem.at[k])

    for cp in small:
        cp.wait()
    for n in range(1, 3):
        load(n).start()
    weights = weight[...].astype(F32)
    row_id = lax.broadcasted_iota(jnp.int32, (16, 5120), 0)
    extra = jnp.where(row_id == 0, 1.0, 0.0)
    scaled = []
    for f in range(2):
        frame = 2 * slab + f
        end = jnp.int32(0)
        shift, scale = mod[0, 0:1, :], mod[1, 0:1, :]
        for clip in range(1, clip_ref.shape[0]):
            end = end + clip_ref[clip - 1]
            later = frame >= end
            shift = jnp.where(later, mod[0, clip : clip + 1, :], shift)
            scale = jnp.where(later, mod[1, clip : clip + 1, :], scale)
        scaled.append((weights * (1.0 + scale)).astype(BF16))
        coarse = shift.astype(BF16).astype(F32)
        extra = jnp.where(row_id == 2 * f + 1, coarse, extra)
        extra = jnp.where(row_id == 2 * f + 2, shift - coarse, extra)
    aux[...] = extra.astype(BF16)
    contract = (((1,), (1,)), ((), ()))
    scaled = jnp.concatenate(scaled, axis=0)
    ones = jnp.ones((128, 128), BF16)
    for k in range(40):
        rhs[128 * k : 128 * k + 128, 0:128] = scaled[:, 128 * k : 128 * k + 128].T
        rhs[128 * k : 128 * k + 128, 128:256] = ones
    col_sum = jnp.dot(aux[...], rhs[...], preferred_element_type=F32)[0:1, 0:128]
    sums = lax.dot_general(aux[...], weight[...], contract, preferred_element_type=F32)
    head_bias = bias_ref[...].reshape(1, 64)
    offset = jnp.concatenate(
        [sums[1:2] + sums[2:3] + head_bias, sums[3:4] + sums[4:5] + head_bias], axis=1
    )

    grid[...] = jnp.zeros_like(grid)
    lane8 = lax.broadcasted_iota(jnp.int32, (8, 128), 1)

    def settle(n):
        pivot, second = moments[0], moments[1]
        mean = raw[:, 128:256] * (1.0 / 5120.0)
        gap = mean - pivot
        var = jnp.sum(second, axis=1, keepdims=True) * (1.0 / 5120.0) - gap * gap
        value = lax.rsqrt(var + 1e-06) * (raw[:, 0:128] - mean * col_sum) + offset
        for m in range(20):
            q = 4 * n + m // 5
            own = (lane8 < 64) == (q < 10)
            row = lax.rem(q, 10) * 56 + 8 + (m % 5) * 8
            at = pl.ds(pl.multiple_of(row, 8), 8)
            grid[at, :] = jnp.where(own, value[8 * m : 8 * m + 8], grid[at, :])

    def head_step(n, carry):
        load(n).wait()

        @pl.when(n < 2)
        def _():
            load(n + 3).start()

        settle(jnp.maximum(n - 1, 0))
        sample = jnp.sum(tokens[n, :, 0:128].astype(F32), axis=1, keepdims=True) * (1.0 / 128.0)
        pivot = jnp.broadcast_to(sample, (160, 128))
        moments[0] = pivot
        for k in range(10):
            at = slice(16 * k, 16 * k + 16)
            second = jnp.zeros((16, 128), F32)
            for tile in range(40):
                v = tokens[n, at, 128 * tile : 128 * tile + 128].astype(F32) - pivot[at]
                second = second + v * v
            moments[1, at] = second
        raw[...] = jnp.dot(tokens[n], rhs[...], preferred_element_type=F32)
        return carry

    lax.fori_loop(0, 5, head_step, 0)
    for k in range(2):
        load_taps(k).start()
    settle(4)

    for j in range(8):
        for pair in range(5):
            pieces = []
            for q in (2 * pair, 2 * pair + 1):
                at = 56 * q + 7 + 5 * j
                pieces.append(grid[at : at + 8, :])
            outgoing[j, 16 * pair : 16 * pair + 16, :] = jnp.concatenate(pieces, axis=0).astype(
                BF16
            )

    def send(d, o):
        to = lax.rem(band + o, bands)
        return pltpu.make_async_remote_copy(
            src_ref=outgoing.at[to],
            dst_ref=recv_ref.at[2 - d, band],
            send_sem=send_sem.at[d, o],
            recv_sem=recv_sem.at[d, o],
            device_id=(slab + d, to),
            device_id_type=MESH,
        )

    pl.semaphore_wait(
        barrier,
        bands * jnp.minimum(slabs - slab, 3) - 1,
    )
    for d in (2, 1, 0):

        @pl.when(slab + d < slabs)
        def _():
            for o in range(1, bands + 1):
                if d or o < bands:
                    send(d, o % bands).start()

    own_copy = pltpu.make_async_copy(outgoing.at[band], recv_ref.at[2, band], small_sem.at[0])
    own_copy.start()

    win_copy.wait()
    blank = jnp.zeros((16, 384), BF16)
    half = jnp.asarray(0.5, BF16)
    for a in range(3):
        for rr in range(4):
            for slot in range(4):
                for p in range(2):
                    for s in range(2):
                        b, e = rr - p, slot - s
                        ok = 0 <= b < 3 and 0 <= e < 3
                        row = a * 256 + rr * 64 + slot * 16
                        col = (2 * p + s) * 384
                        dense_in[row : row + 16, col : col + 384] = (
                            win[9 * a + 3 * b + e] * half if ok else blank
                        )
    dense_store = pltpu.make_async_copy(dense_in, dense_ref, store_sem.at[3])
    dense_store.start()

    second_frame = 2 * slab + 1
    starts = second_frame == 0
    end = jnp.int32(0)
    for clip in range(clip_ref.shape[0] - 1):
        end = end + clip_ref[clip]
        starts = jnp.logical_or(starts, second_frame == end)

    def store_mixed(k):
        at = pl.ds(3 * k, 3)
        return pltpu.make_async_copy(mixed.at[:, at], mixed_ref.at[:, at], store_sem.at[k])

    def mix(k, carry):
        w0, w1, w2 = (taps[a, k].astype(F32) for a in range(3))
        outer = w0 + w2
        mixed[0, k] = jnp.where(starts, taps[1, k], (outer + w1).astype(BF16))
        mixed[1, k] = jnp.where(starts, taps[2, k], (outer - w1).astype(BF16))
        return carry

    for k in range(3):
        load_taps(k).wait()
        if k == 0:
            load_taps(2).start()
        lax.fori_loop(3 * k, 3 * k + 3, mix, 0)
        store_mixed(k).start()

    own_copy.wait()
    for d in range(3):

        @pl.when(slab + d < slabs)
        def _():
            for o in range(bands):
                if d or o:
                    send(d, o).wait_send()

        @pl.when(slab >= d)
        def _():
            for o in range(bands):
                if d or o:
                    send(d, o).wait_recv()

    dense_store.wait()
    for k in range(3):
        store_mixed(k).wait()


def head(
    clip_lengths, hidden, modulation, head_weight, head_bias, conv_in_weight, conv_out_weight
):
    return pl.pallas_call(
        head_kernel,
        out_shape=(
            jax.ShapeDtypeStruct((3, 8, 80, 128), BF16),
            jax.ShapeDtypeStruct((768, 1536), BF16),
            jax.ShapeDtypeStruct((2, 9, 384, 384), BF16),
        ),
        in_specs=[
            pl.BlockSpec(memory_space=pltpu.SMEM),
            pl.BlockSpec(memory_space=pl.ANY),
            pl.BlockSpec(memory_space=pl.ANY),
            pl.BlockSpec(memory_space=pl.ANY),
            pl.BlockSpec(memory_space=pltpu.VMEM),
            pl.BlockSpec(memory_space=pl.ANY),
            pl.BlockSpec(memory_space=pl.ANY),
        ],
        out_specs=[pl.BlockSpec(memory_space=pl.ANY)] * 3,
        scratch_shapes=[
            pltpu.VMEM((5, 160, 5120), BF16),
            pltpu.VMEM((2, 4, 5120), F32),
            pltpu.VMEM((64, 5120), BF16),
            pltpu.VMEM((5120, 256), BF16),
            pltpu.VMEM((16, 5120), BF16),
            pltpu.VMEM((160, 256), F32),
            pltpu.VMEM((2, 160, 128), F32),
            pltpu.VMEM((560, 128), F32),
            pltpu.VMEM((8, 80, 128), BF16),
            pltpu.VMEM((27, 16, 384), BF16),
            pltpu.VMEM((768, 1536), BF16),
            pltpu.VMEM((3, 9, 384, 384), BF16),
            pltpu.VMEM((2, 9, 384, 384), BF16),
            pltpu.SemaphoreType.DMA((5,)),
            pltpu.SemaphoreType.DMA((3,)),
            pltpu.SemaphoreType.DMA((3,)),
            pltpu.SemaphoreType.DMA((4,)),
            pltpu.SemaphoreType.DMA((3, 8)),
            pltpu.SemaphoreType.DMA((3, 8)),
        ],
        compiler_params=pltpu.CompilerParams(
            collective_id=0, has_side_effects=True, vmem_limit_bytes=60 << 20
        ),
    )(
        clip_lengths,
        hidden.transpose(0, 2, 1, 3).reshape(800, 5120),
        modulation,
        head_weight.T,
        head_bias,
        conv_in_weight.reshape(27, 16, 384),
        conv_out_weight.reshape(3, 9, 384, 384),
    )


def on_device(
    hidden, modulation, clip_lengths, head_weight, head_bias,
    conv_in_weight, conv_in_bias, conv_out_weight, conv_out_bias,
):
    received, dense_in, mixed = head(
        clip_lengths, hidden, modulation, head_weight, head_bias, conv_in_weight, conv_out_weight
    )
    return convolve(
        clip_lengths, received, dense_in, conv_in_bias, conv_out_weight, mixed, conv_out_bias
    )


def solution(mesh):
    return jax.shard_map(
        on_device,
        mesh=mesh,
        in_specs=(P("tm", None, "height", None), P(), P(), P(), P(), P(), P(), P(), P()),
        out_specs=P("tm", "height", None, None),
        check_vma=False,
    )
```

```python
import functools

import jax
import jax.numpy as jnp
from jax import lax
from jax.experimental import pallas as pl
from jax.experimental.pallas import tpu as pltpu
from jax.sharding import PartitionSpec as P

F32 = jnp.float32
BF16 = jnp.bfloat16
MESH = pl.DeviceIdType.MESH


def clip_start(clip_ref, frame):
    first = jnp.int32(0)
    end = jnp.int32(0)
    for clip in range(clip_ref.shape[0] - 1):
        end = end + clip_ref[clip]
        first = jnp.where(frame >= end, end, first)
    return first


def conv_kernel(
    clip_ref, recv_ref, win_ref, bin_ref, wout_ref, mixed_ref, bout_ref, out_ref,
    received, win, spread, tokens, dense_in, inner, weights, total, stage, packed,
    recv_sem, load_sem, store_sem, *, rows_per_step,
):
    slab = lax.axis_index("tm")
    band = lax.axis_index("height")
    frame0 = 2 * slab

    recv_copy = pltpu.make_async_copy(recv_ref, received, recv_sem)
    win_copy = pltpu.make_async_copy(win_ref, win, load_sem.at[4])
    win_copy.start()
    recv_copy.start()
    sources = (
        wout_ref.at[pl.ds(0, 9)], mixed_ref.at[0], mixed_ref.at[1], wout_ref.at[pl.ds(18, 9)]
    )
    loads = [
        pltpu.make_async_copy(sources[i], weights.at[i], load_sem.at[i]) for i in range(4)
    ]

    win_copy.wait()
    blank = jnp.zeros((16, 384), BF16)
    half = jnp.asarray(0.5, BF16)
    for a in range(3):
        for rr in range(4):
            for slot in range(4):
                for p in range(2):
                    for s in range(2):
                        b, e = rr - p, slot - s
                        ok = 0 <= b < 3 and 0 <= e < 3
                        row = a * 256 + rr * 64 + slot * 16
                        col = (2 * p + s) * 384
                        dense_in[row : row + 16, col : col + 384] = (
                            win[9 * a + 3 * b + e] * half if ok else blank
                        )
    lane_in = lax.broadcasted_iota(jnp.int32, (128, 256), 0)
    lane_out = lax.broadcasted_iota(jnp.int32, (128, 256), 1)
    wanted = (
        (lane_out // 128) * 64
        + ((lane_out // 64) % 2) * 32
        + ((lane_out // 16 + 1) % 2) * 16
        + lane_out % 16
    )
    spreader = jnp.where(lane_in == wanted, 1.0, 0.0).astype(BF16)
    slot_id = (lax.broadcasted_iota(jnp.int32, (7, 10, 8, 128), 3) // 16) % 4
    group_id = lax.broadcasted_iota(jnp.int32, (7, 1, 8, 128), 2)
    recv_copy.wait()
    for i in (1, 2, 0, 3):
        loads[i].start()
    for back in range(3):
        for src in range(8):
            block = received[back, src].astype(F32)
            for col in range(10):
                spread[back, pl.ds(8 * col + src, 8, stride=80), :] = block[8 * col : 8 * col + 8]
    for back in range(3):
        both = jnp.dot(spread[back, 0:560, :].astype(BF16), spreader, preferred_element_type=F32)
        for f in range(2):
            here = both[:, 128 * f : 128 * f + 128].reshape(7, 10, 8, 128)
            last = pltpu.roll(here[:, 9:10].reshape(56, 128), 1, 0).reshape(7, 1, 8, 128)
            last = jnp.where(group_id == 0, 0.0, last)
            head = pltpu.roll(here[:, 0:1].reshape(56, 128), 55, 0).reshape(7, 1, 8, 128)
            head = jnp.where(group_id == 7, 0.0, head)
            before = jnp.concatenate([last, here[:, 0:9]], axis=1)
            after = jnp.concatenate([here[:, 1:10], head], axis=1)
            mixed_slots = jnp.where(slot_id == 0, before, jnp.where(slot_id == 3, after, here))
            tokens[2 * back + f] = mixed_slots.reshape(560, 128).astype(BF16)

    keep = []
    for g in range(4):
        first = clip_start(clip_ref, frame0 - 2 + g)
        keep.append([frame0 - 4 + g + a >= first for a in range(3)])
    first0 = clip_start(clip_ref, frame0)
    use0 = frame0 - 2 >= first0
    use1 = frame0 - 1 >= first0
    joined = frame0 >= clip_start(clip_ref, frame0 + 1)
    c = jnp.where(joined, 1.0, 0.0).astype(F32)
    c16 = c.astype(BF16)
    halved = jnp.where(joined, 0.5, 1.0).astype(F32)
    paired = jnp.where(joined, 0.5, 0.0).astype(F32)
    bias_in = 0.5 * bin_ref[...].reshape(1, 384)
    bias_in = jnp.concatenate([bias_in, bias_in], axis=1)

    def in_step(step):
        i0 = 2 * step
        for p in range(2):
            x = []
            for g in range(4):
                parts = []
                for a in range(3):
                    lo = tokens[g + a, pl.ds(i0 * 80, 160), :]
                    hi = tokens[g + a, pl.ds(i0 * 80 + 80, 160), :]
                    both = jnp.concatenate([lo, hi], axis=1)
                    if a < 2:
                        both = jnp.where(keep[g][a], both, jnp.zeros_like(both))
                    parts.append(both)
                v = jnp.dot(
                    jnp.concatenate(parts, axis=1),
                    dense_in[:, 768 * p : 768 * p + 768],
                    preferred_element_type=F32,
                )
                v = v + bias_in
                x.append((v + v * jnp.tanh(v)).astype(BF16))
            zero = jnp.zeros_like(x[0])
            x0 = jnp.where(use0, x[0], zero)
            x1 = jnp.where(use1, x[1], zero)
            x2, x3 = x[2], x[3]
            x1c, x2c = c16 * x1, c16 * x2
            sums = (x0 - x2c, x1 + x2c, x2 - x1c, x3 - x1c)
            for r in range(2):
                for i in range(4):
                    inner[i, 4 * step + 2 * r + p] = sums[i][80 * r : 80 * r + 80]

    for step in range(3):
        in_step(step)

    @pl.when(band == 0)
    def _():
        inner[:, 0] = jnp.zeros((4, 80, 768), BF16)

    @pl.when(band == 7)
    def _():
        inner[:, 11] = jnp.zeros((4, 80, 768), BF16)

    for cp in loads:
        cp.wait()

    R = rows_per_step
    rows = 80 * R
    bias_out = bout_ref[...].reshape(1, 384)
    group_out = lax.broadcasted_iota(jnp.int32, (R, 1, 8, 384), 2)

    def weight(i, b, e):
        return weights[i, 3 * b + e]

    def product(i, h0):
        taps = [inner[i, pl.ds(h0 + b, R)].reshape(rows, 768) for b in range(3)]
        main_w = jnp.concatenate(
            [
                jnp.concatenate(
                    [
                        jnp.concatenate([weight(i, b, 1), weight(i, b, 0)], axis=1),
                        jnp.concatenate([weight(i, b, 2), weight(i, b, 1)], axis=1),
                    ],
                    axis=0,
                )
                for b in range(3)
            ],
            axis=0,
        )
        main = jnp.dot(jnp.concatenate(taps, axis=1), main_w, preferred_element_type=F32)
        left = jnp.dot(
            jnp.concatenate([tap[:, 384:] for tap in taps], axis=1),
            jnp.concatenate([weight(i, b, 0) for b in range(3)], axis=0),
            preferred_element_type=F32,
        )
        right = jnp.dot(
            jnp.concatenate([tap[:, :384] for tap in taps], axis=1),
            jnp.concatenate([weight(i, b, 2) for b in range(3)], axis=0),
            preferred_element_type=F32,
        )
        return (main, left, right)

    def finish(f, h0, main, left, right):
        left = left.reshape(R, 10, 8, 384)
        last = pltpu.roll(left[:, 9:10].reshape(8 * R, 384), 1, 0).reshape(R, 1, 8, 384)
        last = jnp.where(group_out == 0, 0.0, last)
        left = jnp.concatenate([last, left[:, 0:9]], axis=1).reshape(rows, 384)
        right = right.reshape(R, 10, 8, 384)
        head = pltpu.roll(right[:, 0:1].reshape(8 * R, 384), 8 * R - 1, 0).reshape(R, 1, 8, 384)
        head = jnp.where(group_out == 7, 0.0, head)
        right = jnp.concatenate([right[:, 1:10], head], axis=1).reshape(rows, 384)
        halves = (main[:, :384] + left + bias_out, main[:, 384:] + right + bias_out)
        for r in range(R):
            for s in range(2):
                for col in range(10):
                    at = 80 * r + 8 * col
                    for lane in range(3):
                        stage[f, 3 * r + lane, pl.ds(2 * col + s, 8, stride=20), :] = halves[s][
                            at : at + 8, 128 * lane : 128 * lane + 128
                        ]
        for r in range(R):
            for lane in range(3):
                packed[f, h0 + r, :, 128 * lane : 128 * lane + 128] = stage[
                    f, 3 * r + lane
                ].astype(BF16)

    def store(f, h0):
        return pltpu.make_async_copy(
            packed.at[f, pl.ds(h0, R)], out_ref.at[f, pl.ds(h0, R)], store_sem.at[f]
        )

    at = (0, 768, 1152, 1536)

    def finish_one(f, h0):
        finish(f, h0, *[total[f, :, at[n] : at[n + 1]] for n in range(3)])

    for h0 in range(0, 10, R):
        if h0 > 0:
            for f in range(2):
                finish_one(f, h0 - R)
        m1 = product(1, h0)
        m2 = product(2, h0)
        m0 = product(0, h0)
        for n, (u, v, w) in enumerate(zip(m0, m1, m2)):
            total[0, :, at[n] : at[n + 1]] = u + halved * (v + w)
            total[1, :, at[n] : at[n + 1]] = paired * (v - w)
        if h0 + R == 10:
            finish_one(0, h0)
        for n, u in enumerate(product(3, h0)):
            total[1, :, at[n] : at[n + 1]] = total[1, :, at[n] : at[n + 1]] + u
        if h0 > 0:
            for f in range(2):
                store(f, h0 - R).start()
    store(0, 10 - R).start()
    finish_one(1, 10 - R)
    store(1, 10 - R).start()
    for f in range(2):
        pltpu.make_async_copy(packed.at[f], out_ref.at[f], store_sem.at[f]).wait()


def convolve(
    clip_lengths, received, conv_in_weight, conv_in_bias, conv_out_weight, mixed, conv_out_bias,
    rows_per_step=2,
):
    R = rows_per_step
    return pl.pallas_call(
        functools.partial(conv_kernel, rows_per_step=R),
        out_shape=jax.ShapeDtypeStruct((2, 10, 160, 384), BF16),
        in_specs=[
            pl.BlockSpec(memory_space=pltpu.SMEM),
            pl.BlockSpec(memory_space=pl.ANY),
            pl.BlockSpec(memory_space=pl.ANY),
            pl.BlockSpec(memory_space=pltpu.VMEM),
            pl.BlockSpec(memory_space=pl.ANY),
            pl.BlockSpec(memory_space=pl.ANY),
            pl.BlockSpec(memory_space=pltpu.VMEM),
        ],
        out_specs=pl.BlockSpec(memory_space=pl.ANY),
        scratch_shapes=[
            pltpu.VMEM((3, 8, 80, 128), BF16),
            pltpu.VMEM((27, 16, 384), BF16),
            pltpu.VMEM((3, 640, 128), F32),
            pltpu.VMEM((6, 560, 128), BF16),
            pltpu.VMEM((768, 1536), BF16),
            pltpu.VMEM((4, 12, 80, 768), BF16),
            pltpu.VMEM((4, 9, 384, 384), BF16),
            pltpu.VMEM((2, 80 * R, 1536), F32),
            pltpu.VMEM((2, 3 * R, 160, 128), F32),
            pltpu.VMEM((2, 10, 160, 384), BF16),
            pltpu.SemaphoreType.DMA,
            pltpu.SemaphoreType.DMA((5,)),
            pltpu.SemaphoreType.DMA((2,)),
        ],
        compiler_params=pltpu.CompilerParams(vmem_limit_bytes=60 << 20),
    )(
        clip_lengths, received, conv_in_weight.reshape(27, 16, 384), conv_in_bias,
        conv_out_weight.reshape(27, 384, 384), mixed, conv_out_bias,
    )


def head_kernel(
    clip_ref, hidden_ref, mod_ref, weight_ref, bias_ref, wout_ref, recv_ref, mixed_ref,
    tokens, mod, weight, rhs, aux, raw, moments, grid, outgoing, taps, mixed,
    load_sem, small_sem, tap_sem, store_sem, send_sem, recv_sem,
):
    slab = lax.axis_index("tm")
    band = lax.axis_index("height")
    slabs = lax.axis_size("tm")
    bands = lax.axis_size("height")
    small = [
        pltpu.make_async_copy(weight_ref, weight, small_sem.at[0]),
        pltpu.make_async_copy(mod_ref, mod, small_sem.at[1]),
    ]
    for cp in small:
        cp.start()

    def load(n):
        return pltpu.make_async_copy(
            hidden_ref.at[pl.ds(pl.multiple_of(160 * n, 16), 160)], tokens.at[n], load_sem.at[n]
        )

    for n in range(1):
        load(n).start()

    barrier = pltpu.get_barrier_semaphore()
    for d in range(3):

        @pl.when(slab >= d)
        def _():
            for o in range(bands):
                if d or o:
                    source = (slab - d, lax.rem(band + bands - o, bands))
                    pl.semaphore_signal(barrier, inc=1, device_id=source, device_id_type=MESH)

    def load_taps(k):
        at = pl.ds(3 * k, 3)
        return pltpu.make_async_copy(wout_ref.at[:, at], taps.at[:, at], tap_sem.at[k])

    for cp in small:
        cp.wait()
    for n in range(1, 3):
        load(n).start()
    weights = weight[...].astype(F32)
    row_id = lax.broadcasted_iota(jnp.int32, (16, 5120), 0)
    extra = jnp.where(row_id == 0, 1.0, 0.0)
    scaled = []
    for f in range(2):
        frame = 2 * slab + f
        end = jnp.int32(0)
        shift, scale = mod[0, 0:1, :], mod[1, 0:1, :]
        for clip in range(1, clip_ref.shape[0]):
            end = end + clip_ref[clip - 1]
            later = frame >= end
            shift = jnp.where(later, mod[0, clip : clip + 1, :], shift)
            scale = jnp.where(later, mod[1, clip : clip + 1, :], scale)
        scaled.append((weights * (1.0 + scale)).astype(BF16))
        coarse = shift.astype(BF16).astype(F32)
        extra = jnp.where(row_id == 2 * f + 1, coarse, extra)
        extra = jnp.where(row_id == 2 * f + 2, shift - coarse, extra)
    aux[...] = extra.astype(BF16)
    contract = (((1,), (1,)), ((), ()))
    scaled = jnp.concatenate(scaled, axis=0)
    ones = jnp.ones((128, 128), BF16)
    for k in range(40):
        rhs[128 * k : 128 * k + 128, 0:128] = scaled[:, 128 * k : 128 * k + 128].T
        rhs[128 * k : 128 * k + 128, 128:256] = ones
    col_sum = jnp.dot(aux[...], rhs[...], preferred_element_type=F32)[0:1, 0:128]
    sums = lax.dot_general(aux[...], weight[...], contract, preferred_element_type=F32)
    head_bias = bias_ref[...].reshape(1, 64)
    offset = jnp.concatenate(
        [sums[1:2] + sums[2:3] + head_bias, sums[3:4] + sums[4:5] + head_bias], axis=1
    )

    grid[...] = jnp.zeros_like(grid)
    lane8 = lax.broadcasted_iota(jnp.int32, (8, 128), 1)

    def settle(n):
        pivot, second = moments[0], moments[1]
        mean = raw[:, 128:256] * (1.0 / 5120.0)
        gap = mean - pivot
        var = jnp.sum(second, axis=1, keepdims=True) * (1.0 / 5120.0) - gap * gap
        value = lax.rsqrt(var + 1e-06) * (raw[:, 0:128] - mean * col_sum) + offset
        for m in range(20):
            q = 4 * n + m // 5
            own = (lane8 < 64) == (q < 10)
            row = lax.rem(q, 10) * 56 + 8 + (m % 5) * 8
            at = pl.ds(pl.multiple_of(row, 8), 8)
            grid[at, :] = jnp.where(own, value[8 * m : 8 * m + 8], grid[at, :])

    def head_step(n, carry):
        load(n).wait()

        @pl.when(n < 2)
        def _():
            load(n + 3).start()

        settle(jnp.maximum(n - 1, 0))
        sample = jnp.sum(tokens[n, :, 0:128].astype(F32), axis=1, keepdims=True) * (1.0 / 128.0)
        pivot = jnp.broadcast_to(sample, (160, 128))
        moments[0] = pivot
        for k in range(10):
            at = slice(16 * k, 16 * k + 16)
            second = jnp.zeros((16, 128), F32)
            for tile in range(40):
                v = tokens[n, at, 128 * tile : 128 * tile + 128].astype(F32) - pivot[at]
                second = second + v * v
            moments[1, at] = second
        raw[...] = jnp.dot(tokens[n], rhs[...], preferred_element_type=F32)
        return carry

    lax.fori_loop(0, 5, head_step, 0)
    settle(4)

    for j in range(8):
        for pair in range(5):
            pieces = []
            for q in (2 * pair, 2 * pair + 1):
                at = 56 * q + 7 + 5 * j
                pieces.append(grid[at : at + 8, :])
            outgoing[j, 16 * pair : 16 * pair + 16, :] = jnp.concatenate(pieces, axis=0).astype(
                BF16
            )

    def send(d, o):
        to = lax.rem(band + o, bands)
        return pltpu.make_async_remote_copy(
            src_ref=outgoing.at[to],
            dst_ref=recv_ref.at[2 - d, band],
            send_sem=send_sem.at[d, o],
            recv_sem=recv_sem.at[d, o],
            device_id=(slab + d, to),
            device_id_type=MESH,
        )

    pl.semaphore_wait(
        barrier,
        bands * jnp.minimum(slabs - slab, 3) - 1,
    )
    for d in (2, 1, 0):

        @pl.when(slab + d < slabs)
        def _():
            for o in (4, 5, 3, 6, 2, 7, 1, 0):
                if d or o:
                    send(d, o).start()

    own_copy = pltpu.make_async_copy(outgoing.at[band], recv_ref.at[2, band], small_sem.at[0])
    own_copy.start()

    for k in range(2):
        load_taps(k).start()

    second_frame = 2 * slab + 1
    starts = second_frame == 0
    end = jnp.int32(0)
    for clip in range(clip_ref.shape[0] - 1):
        end = end + clip_ref[clip]
        starts = jnp.logical_or(starts, second_frame == end)

    def store_mixed(k):
        at = pl.ds(3 * k, 3)
        return pltpu.make_async_copy(mixed.at[:, at], mixed_ref.at[:, at], store_sem.at[k])

    def mix(k, carry):
        w0, w1, w2 = (taps[a, k].astype(F32) for a in range(3))
        outer = w0 + w2
        mixed[0, k] = jnp.where(starts, taps[1, k], (outer + w1).astype(BF16))
        mixed[1, k] = jnp.where(starts, taps[2, k], (outer - w1).astype(BF16))
        return carry

    for k in range(3):
        load_taps(k).wait()
        if k == 0:
            load_taps(2).start()
        lax.fori_loop(3 * k, 3 * k + 3, mix, 0)
        store_mixed(k).start()

    own_copy.wait()
    for d in range(3):

        @pl.when(slab + d < slabs)
        def _():
            for o in range(bands):
                if d or o:
                    send(d, o).wait_send()

        @pl.when(slab >= d)
        def _():
            for o in range(bands):
                if d or o:
                    send(d, o).wait_recv()

    for k in range(3):
        store_mixed(k).wait()


def head(
    clip_lengths, hidden, modulation, head_weight, head_bias, conv_out_weight
):
    return pl.pallas_call(
        head_kernel,
        out_shape=(
            jax.ShapeDtypeStruct((3, 8, 80, 128), BF16),
            jax.ShapeDtypeStruct((2, 9, 384, 384), BF16),
        ),
        in_specs=[
            pl.BlockSpec(memory_space=pltpu.SMEM),
            pl.BlockSpec(memory_space=pl.ANY),
            pl.BlockSpec(memory_space=pl.ANY),
            pl.BlockSpec(memory_space=pl.ANY),
            pl.BlockSpec(memory_space=pltpu.VMEM),
            pl.BlockSpec(memory_space=pl.ANY),
        ],
        out_specs=[pl.BlockSpec(memory_space=pl.ANY)] * 2,
        scratch_shapes=[
            pltpu.VMEM((5, 160, 5120), BF16),
            pltpu.VMEM((2, 4, 5120), F32),
            pltpu.VMEM((64, 5120), BF16),
            pltpu.VMEM((5120, 256), BF16),
            pltpu.VMEM((16, 5120), BF16),
            pltpu.VMEM((160, 256), F32),
            pltpu.VMEM((2, 160, 128), F32),
            pltpu.VMEM((560, 128), F32),
            pltpu.VMEM((8, 80, 128), BF16),
            pltpu.VMEM((3, 9, 384, 384), BF16),
            pltpu.VMEM((2, 9, 384, 384), BF16),
            pltpu.SemaphoreType.DMA((5,)),
            pltpu.SemaphoreType.DMA((3,)),
            pltpu.SemaphoreType.DMA((3,)),
            pltpu.SemaphoreType.DMA((4,)),
            pltpu.SemaphoreType.DMA((3, 8)),
            pltpu.SemaphoreType.DMA((3, 8)),
        ],
        compiler_params=pltpu.CompilerParams(
            collective_id=0, has_side_effects=True, vmem_limit_bytes=60 << 20
        ),
    )(
        clip_lengths,
        hidden.transpose(0, 2, 1, 3).reshape(800, 5120),
        modulation,
        head_weight.T,
        head_bias,
        conv_out_weight.reshape(3, 9, 384, 384),
    )


def on_device(
    hidden, modulation, clip_lengths, head_weight, head_bias,
    conv_in_weight, conv_in_bias, conv_out_weight, conv_out_bias,
):
    received, mixed = head(
        clip_lengths, hidden, modulation, head_weight, head_bias, conv_out_weight
    )
    return convolve(
        clip_lengths, received, conv_in_weight, conv_in_bias, conv_out_weight, mixed, conv_out_bias
    )


def solution(mesh):
    return jax.shard_map(
        on_device,
        mesh=mesh,
        in_specs=(P("tm", None, "height", None), P(), P(), P(), P(), P(), P(), P(), P()),
        out_specs=P("tm", "height", None, None),
        check_vma=False,
    )
```
